256 devices in a mesh: dp: 4 (over x), section: 4 (over y_lo, core), mp: 16 (over y_hi, z).
Axes of the slice: x: 4, y: 4 (y_hi: 2, y_lo: 2; y = y_hi * 2 + y_lo), z: 8, core: 2. Of those that a mesh axis runs over, the one named last changes fastest.
Arguments:
- layer_input: bfloat16 [4, 1024, 2048], P('section', 'dp'), may hold values from -6 to 6
- top_grad: bfloat16 [1024, 2048], P('dp'), may hold values from -6 to 6
- norm_gain: float32 [4, 2048], P('section'), may hold values from 0.25 to 1.75
- gate_weight: bfloat16 [4, 2048, 8192], P('section', None, 'mp'), may hold values from -0.125 to 0.125
- up_weight: bfloat16 [4, 2048, 8192], P('section', None, 'mp'), may hold values from -0.125 to 0.125
- down_weight: bfloat16 [4, 8192, 2048], P('section', 'mp'), may hold values from -0.0625 to 0.0625
- first_moment: float32 [4, 2048, 8192], P('section', 'dp', 'mp'), may hold values from -96 to 96
- second_moment: float32 [4, 2048, 8192], P('section', 'dp', 'mp'), may hold values from 16 to 1024
Outputs:
- input_grad: bfloat16 [4, 1024, 2048], P('section', 'dp')
- gate_grad: bfloat16 [4, 2048, 8192], P('section', 'dp', 'mp')
- up_grad: bfloat16 [4, 2048, 8192], P('section', 'dp', 'mp')
- adam_step: float32 [4, 2048, 8192], P('section', 'dp', 'mp')
The draws below stay inside these ranges and needn't reach their ends.
All inputs are finite; a program needn't handle non-finite values.
Results may differ from the reference program's by a relative error of at most 0.035.
Values may be sent and summed in bfloat16 or wider, within the bound.
A program may use at most 128 MiB of HBM per device.

```python
import math
import jax
import jax.numpy as jnp
from jax import lax

D = 2048
FF = 8192
TOKENS = 1024
SECTIONS = 4
N_MP = 16


def block_scale(stream_key, shape, shards, smallest, high):
    def one(dim, parts):
        steps = jax.random.uniform(jax.random.fold_in(jax.random.fold_in(stream_key, 6), dim), (parts,), jnp.float32, smallest / len(shards), high / len(shards))
        return jnp.repeat(jnp.exp(steps), shape[dim] // parts).reshape((-1,) + (1,) * (len(shape) - dim - 1))

    factor_of = one(*shards[0])
    for cut in shards[1:]:
        factor_of = factor_of * one(*cut)
    return factor_of


def noise(rng, shape, width, reach, shards=(), dtype=jnp.bfloat16):
    loudness = block_scale(rng, shape, shards, -0.22, 0.18) if shards else 1.0
    array = jax.random.normal(rng, shape, jnp.float32) * width * loudness
    return jnp.minimum(jnp.maximum(array, -reach), reach).astype(dtype)


def setup_inputs(seed: int = 0) -> dict:
    key_list = jax.random.split(jax.random.key(seed), 9)
    layer_input = noise(key_list[0], (SECTIONS, TOKENS, D), 1.0, 6.0, ((0, 4), (1, 4)))
    top_grad = noise(key_list[1], (TOKENS, D), 1.0, 6.0, ((0, 4),))
    norm_gain = jnp.clip(1.0 + 0.15 * jax.random.normal(key_list[2], (SECTIONS, D), jnp.float32), 0.25, 1.75)
    gate_weight = noise(key_list[3], (SECTIONS, D, FF), D ** -0.5, 0.125, ((0, 4), (2, 16)))
    up_weight = noise(key_list[4], (SECTIONS, D, FF), D ** -0.5, 0.125, ((0, 4), (2, 16)))
    down_weight = noise(key_list[5], (SECTIONS, FF, D), FF ** -0.5, 0.0625, ((0, 4), (1, 16)))
    first_moment = noise(key_list[6], (SECTIONS, D, FF), 16.0, 96.0, ((0, 4), (1, 4), (2, 16)), jnp.float32)
    second_moment = jnp.clip(jnp.exp(math.log(1024.0) - 4.158883 * jax.random.uniform(key_list[7], (SECTIONS, D, FF), jnp.float32) ** block_scale(key_list[7], (SECTIONS, D, FF), ((0, 4), (1, 4), (2, 16)), -0.2, 0.2)), 16.0, 1024.0)
    return {"layer_input": layer_input, "top_grad": top_grad, "norm_gain": norm_gain, "gate_weight": gate_weight, "up_weight": up_weight, "down_weight": down_weight, "first_moment": first_moment, "second_moment": second_moment}


first_fix = 1.0 - 0.9 ** 20
second_fix = 1.0 - 0.95 ** 20

def dot_last(left, right):
    return lax.dot_general(left, right, (((1,), (1,)), ((), ())), preferred_element_type=jnp.float32)

def dot_first(left, right):
    return lax.dot_general(left, right, (((0,), (0,)), ((), ())), preferred_element_type=jnp.float32)

def section_backward(layer_rows, gain_row, gate_w, up_w, down_w, upstream):
    values = layer_rows.astype(jnp.float32)
    scale_inv = lax.rsqrt(lax.optimization_barrier(jnp.mean(values * values, axis=-1, keepdims=True)) + 1e-05)
    normed = values * scale_inv
    normed_gain = (normed * gain_row).astype(jnp.bfloat16)
    gate_pre = jnp.dot(normed_gain, gate_w, preferred_element_type=jnp.float32)
    up_pre = jnp.dot(normed_gain, up_w, preferred_element_type=jnp.float32)
    sigmoid_gate = jax.nn.sigmoid(gate_pre)
    gated = gate_pre * sigmoid_gate
    hidden = (gated * up_pre).astype(jnp.bfloat16)
    grad_hidden = dot_last(upstream, down_w)
    grad_gate = (grad_hidden * up_pre * sigmoid_gate * (1.0 + gate_pre * (1.0 - sigmoid_gate))).astype(jnp.bfloat16)
    grad_up = (grad_hidden * gated).astype(jnp.bfloat16)
    unit_count = FF // N_MP

    def add_block(block_index, summed):
        first_row = block_index * unit_count
        gate_cols = lax.dynamic_slice_in_dim(grad_gate, first_row, unit_count, 1)
        up_cols = lax.dynamic_slice_in_dim(grad_up, first_row, unit_count, 1)
        gate_part = lax.dynamic_slice_in_dim(gate_w, first_row, unit_count, 1)
        up_part = lax.dynamic_slice_in_dim(up_w, first_row, unit_count, 1)
        partial_value = dot_last(gate_cols, gate_part) + dot_last(up_cols, up_part)
        rounded = lax.optimization_barrier(partial_value.astype(jnp.bfloat16))
        return summed + rounded.astype(jnp.float32)
    grad_normed = lax.fori_loop(0, N_MP, add_block, jnp.zeros(upstream.shape, jnp.float32))
    scaled = grad_normed * gain_row
    projection = lax.optimization_barrier(jnp.mean(scaled * normed, axis=-1, keepdims=True))
    sent_grad = (upstream.astype(jnp.float32) + scale_inv * (scaled - normed * projection)).astype(jnp.bfloat16)
    gate_sum = dot_first(normed_gain, grad_gate).astype(jnp.bfloat16)
    up_sum = dot_first(normed_gain, grad_up).astype(jnp.bfloat16)
    down_sum = dot_first(upstream, hidden)
    return (sent_grad, gate_sum, up_sum, down_sum)

def reference(layer_input, top_grad, norm_gain, gate_weight, up_weight, down_weight, first_moment, second_moment):
    upstream = top_grad
    sent_list, gate_list, up_list, step_list = ([], [], [], [])
    for layer in range(SECTIONS - 1, -1, -1):
        sent_grad, gate_sum, up_sum, down_sum = section_backward(layer_input[layer], norm_gain[layer], gate_weight[layer], up_weight[layer], down_weight[layer], upstream)
        new_first = 0.9 * first_moment[layer] + 0.1 * down_sum
        new_second = 0.95 * second_moment[layer] + 0.05 * down_sum * down_sum
        adam_step = new_first / first_fix / (jnp.sqrt(new_second / second_fix) + 1e-08)
        sent_list.insert(0, sent_grad)
        gate_list.insert(0, gate_sum)
        up_list.insert(0, up_sum)
        step_list.insert(0, adam_step)
        upstream = sent_grad
    return (jnp.stack(sent_list), jnp.stack(gate_list), jnp.stack(up_list), jnp.stack(step_list))
```

```python
import jax
import jax.numpy as jnp
from jax import lax
from jax.experimental import pallas as pl
from jax.experimental.pallas import tpu as pltpu
from jax.sharding import PartitionSpec as P

first_fix = 1.0 - 0.9**20
second_fix = 1.0 - 0.95**20

MESH = pl.DeviceIdType.MESH
F32 = jnp.float32
BF16 = jnp.bfloat16

ROWS = 256
D = 2048
UNITS = 512
HALF = D // 2
CHUNKS = 4
CH = ROWS // CHUNKS
BLOCKS = CH // 8
FAR_FIRST = (4, 3, 5, 2, 6, 1, 7, 0)


def dot_nn(left, right):
    return lax.dot_general(left, right, (((1,), (0,)), ((), ())), preferred_element_type=F32)


def dot_nt(left, right):
    return lax.dot_general(left, right, (((1,), (1,)), ((), ())), preferred_element_type=F32)


def kernel(
    li_h, tg_h, gain_h, gw_h, uw_h, dw_h, fm_h, sm_h,
    ig_o, gg_o, ug_o, ad_o,
    li, w, dw, up, gain, fm, sm,
    ng, gated, slope, gx, hx, ngx, ux, ngt, uxt,
    snd, rsbuf, rout, agbuf, igbuf, ig, gg, ug, ad,
    liown, gnown, incb, tgown,
    ld, rs_r, ag_r, ig_r, li_r, gn_r, inc_r, dp_r,
    rs_s, ag_s, inc_s, li_s, gn_s, fw_s, dp_s, own_s, out_s,
):
    d = lax.axis_index("dp")
    s = lax.axis_index("section")
    m = lax.axis_index("mp")
    yh, z = m // 8, m % 8
    owner = jnp.where(s >= 2, 0, 3)
    turn = 1 - s % 2

    def local(src, dst, sem):
        return pltpu.make_async_copy(src, dst, sem)

    def remote(src, dst, ssem, rsem, **to):
        return pltpu.make_async_remote_copy(src, dst, ssem, rsem, device_id=to, device_id_type=MESH)

    loads = [
        local(li_h.at[0], li, ld.at[0]),
        local(gain_h, gain, ld.at[1]),
        local(gw_h.at[0], w.at[:, pl.ds(0, UNITS)], ld.at[2]),
        local(uw_h.at[0], w.at[:, pl.ds(UNITS, UNITS)], ld.at[3]),
        local(dw_h.at[0], dw, ld.at[4]),
    ]
    late = [local(fm_h.at[0], fm, ld.at[5]), local(sm_h.at[0], sm, ld.at[6])]
    tg_load = local(tg_h, up, ld.at[7])

    def block16(i):
        return pl.ds(pl.multiple_of(CH * (yh + 2 * i) + 16 * (z // 2), 16), 16)

    tg_rows = [local(tg_h.at[block16(i)], tgown.at[i], ld.at[8 + i]) for i in range(2)]

    for cp in loads:
        cp.start()

    @pl.when(s == 3)
    def _():
        tg_load.start()

    @pl.when(s == 0)
    def _():
        for cp in tg_rows:
            cp.start()

    for cp in late:
        cp.start()

    loads[0].wait()
    loads[1].wait()
    li_sends = [
        remote(li.at[block16(i)], liown.at[turn, i], li_s.at[i], li_r.at[turn, i], section=owner)
        for i in range(2)
    ]
    gn_send = remote(gain, gnown.at[turn], gn_s.at[0], gn_r.at[turn], section=owner)
    for cp in li_sends:
        cp.start()
    gn_send.start()

    def norm_rows(j, carry):
        rows = pl.ds(pl.multiple_of(j * 32, 32), 32)
        values = li[rows, :].astype(F32)
        scale_inv = lax.rsqrt(jnp.mean(values * values, axis=-1, keepdims=True) + 1e-05)
        ng[rows, :] = (values * scale_inv * gain[...]).astype(BF16)
        return carry

    lax.fori_loop(0, ROWS // 32, norm_rows, 0)
    loads[2].wait()
    loads[3].wait()

    def forward(j, carry):
        cols = pl.ds(pl.multiple_of(j * 256, 256), 256)
        cols_up = pl.ds(pl.multiple_of(UNITS + j * 256, 256), 256)
        gate_pre = dot_nn(ng[...], w[:, cols])
        up_pre = dot_nn(ng[...], w[:, cols_up])
        sig = jax.nn.sigmoid(gate_pre)
        gate = gate_pre * sig
        gated[:, cols] = gate
        hx[0, :, cols] = (gate * up_pre).astype(BF16)
        slope[:, cols] = up_pre * sig * (1.0 + gate_pre * (1.0 - sig))
        return carry

    lax.fori_loop(0, UNITS // 256, forward, 0)
    loads[4].wait()

    def feature_cols(k):
        return pl.ds(pl.multiple_of(lax.rem(d + k, 4) * 512, 512), 512)

    own_ng = local(ng.at[:, feature_cols(0)], ngx.at[0], own_s.at[0])

    def bulk():
        own_ng.start()
        for k in (2, 1, 3):
            peer = lax.rem(d + k, 4)
            remote(ng.at[:, feature_cols(k)], ngx.at[4 - k], dp_s.at[0], dp_r.at[0], dp=peer).start()
            remote(hx.at[0], hx.at[4 - k], dp_s.at[1], dp_r.at[1], dp=peer).start()

    def reduce_layer(u, i, incoming, sends):
        remote(rsbuf.at[u, i], rsbuf.at[u, i], rs_s.at[0], rs_r.at[u, i], mp=m).wait_recv()
        even = z % 2 == 0
        values = liown[u, i].astype(F32)
        values = jnp.where(even, values[:8], values[8:])
        scale_inv = lax.rsqrt(jnp.mean(values * values, axis=-1, keepdims=True) + 1e-05)
        normed = values * scale_inv
        total = rsbuf[u, i, 0].astype(F32)
        for k in range(1, 16):
            total = total + rsbuf[u, i, k].astype(F32)
        scaled_l = total[:8] * gnown[u, :, pl.ds(0, HALF)]
        scaled_r = total[8:] * gnown[u, :, pl.ds(HALF, HALF)]
        norm_l, norm_r = normed[:, :HALF], normed[:, HALF:]
        both = jnp.sum(scaled_l * norm_l + scaled_r * norm_r, axis=-1, keepdims=True)
        projection = both * (1.0 / D)
        inc_l, inc_r = incoming(i)
        out_l = inc_l + scale_inv * (scaled_l - norm_l * projection)
        out_r = inc_r + scale_inv * (scaled_r - norm_r * projection)
        rout[u, i] = jnp.concatenate([out_l, out_r], axis=0).astype(BF16)
        sends(u, i)

    def halves(block):
        block = block.astype(F32)
        return block[:8], block[8:]

    def gather_to(section, buf, sem):
        def sends(u, i):
            chunk = yh + 2 * i
            for k in FAR_FIRST:
                for h in range(2):
                    to = lax.rem(z + k, 8) + 8 * h
                    remote(
                        rout.at[u, i], buf.at[chunk, z], ag_s.at[u, i], sem.at[chunk], section=section, mp=to
                    ).start()
        return sends

    def own_rows_ready(u):
        for i in range(2):
            remote(liown.at[u, i], liown.at[u, i], li_s.at[0], li_r.at[u, i], mp=m).wait_recv()
        remote(gnown.at[u], gnown.at[u], gn_s.at[0], gn_r.at[u], mp=m).wait_recv()

    def from_rout(i):
        return halves(rout[0, i])

    def wait_gather_sends():
        for u in range(2):
            for i in range(2):
                remote(rsbuf.at[u, i], rsbuf.at[u, i], ag_s.at[u, i], rs_r.at[u, i], mp=m).wait_send()

    @pl.when(s < 3)
    def _():
        bulk()

    @pl.when(s == 0)
    def _():
        for cp in tg_rows:
            cp.wait()
        own_rows_ready(0)
        own_rows_ready(1)

        def from_top(i):
            block = tgown[i].astype(F32)
            rows = jnp.where(z % 2 == 0, block[:8], block[8:])
            return rows[:, :HALF], rows[:, HALF:]

        def sends_two(u, i):
            gather_to(1, agbuf, ag_r)(u, i)
            remote(rout.at[u, i], incb.at[i], inc_s.at[i], inc_r.at[i], section=3).start()

        for i in range(2):
            reduce_layer(0, i, from_top, gather_to(2, agbuf, ag_r))
        for i in range(2):
            reduce_layer(1, i, from_rout, sends_two)

    @pl.when(s == 3)
    def _():
        tg_load.wait()

    below = jnp.where(s == 3, 0, s + 1)

    def unpack(src, c, dst):
        def pair(j, carry):
            a_l, a_r = halves(src[c, 2 * j])
            b_l, b_r = halves(src[c, 2 * j + 1])
            rows = pl.ds(pl.multiple_of(CH * c + 16 * j, 16), 16)
            dst[rows, pl.ds(0, HALF)] = jnp.concatenate([a_l, b_l], axis=0).astype(BF16)
            dst[rows, pl.ds(HALF, HALF)] = jnp.concatenate([a_r, b_r], axis=0).astype(BF16)
            return carry
        lax.fori_loop(0, BLOCKS // 2, pair, 0)

    def chunk_step(c, carry):
        rows = pl.ds(pl.multiple_of(CH * c, CH), CH)

        @pl.when(s < 3)
        def _():
            remote(agbuf.at[c], agbuf.at[c], rs_s.at[0], ag_r.at[c], mp=m).wait_recv()
            unpack(agbuf, c, up)

        grad_hidden = dot_nt(up[rows, :], dw[...])
        gx[0, rows, pl.ds(0, UNITS)] = (grad_hidden * slope[rows, :]).astype(BF16)
        gx[0, rows, pl.ds(UNITS, UNITS)] = (grad_hidden * gated[rows, :]).astype(BF16)

        def tile(t, carry):
            cols = pl.ds(pl.multiple_of(t * 512, 512), 512)
            cols_right = pl.ds(pl.multiple_of(HALF + t * 512, 512), 512)
            left = dot_nt(gx[0, rows, :], w[cols, :])
            right = dot_nt(gx[0, rows, :], w[cols_right, :])
            for b in range(BLOCKS):
                both = jnp.concatenate([left[8 * b : 8 * b + 8], right[8 * b : 8 * b + 8]], axis=0)
                snd[c, b, :, cols] = both.astype(BF16)
            return carry

        lax.fori_loop(0, 2, tile, 0)
        for k in FAR_FIRST:
            to = lax.rem(z + k, 8)
            remote(
                snd.at[c, to], rsbuf.at[turn, c // 2, m], rs_s.at[0], rs_r.at[turn, c // 2],
                section=owner, mp=to + 8 * (c % 2),
            ).start()

        @pl.when(s < 3)
        def _():
            remote(agbuf.at[c], igbuf.at[c], fw_s.at[0], ig_r.at[c], section=below).start()

        local(up.at[rows, feature_cols(0)], ux.at[0, rows], own_s.at[1]).start()
        for k in (2, 1, 3):
            peer = lax.rem(d + k, 4)
            remote(gx.at[0, rows], gx.at[4 - k, rows], dp_s.at[2], dp_r.at[2], dp=peer).start()
            remote(up.at[rows, feature_cols(k)], ux.at[4 - k, rows], dp_s.at[3], dp_r.at[3], dp=peer).start()
        return carry

    lax.fori_loop(0, CHUNKS, chunk_step, 0)

    @pl.when(s == 3)
    def _():
        bulk()
        own_rows_ready(0)
        own_rows_ready(1)
        for i in range(2):
            remote(incb.at[i], incb.at[i], inc_s.at[0], inc_r.at[i], mp=m).wait_recv()

        def from_inc(i):
            return halves(incb[i])

        for i in range(2):
            reduce_layer(0, i, from_inc, gather_to(0, agbuf, ag_r))
        for i in range(2):
            reduce_layer(1, i, from_rout, gather_to(0, igbuf, ig_r))

    others = pl.ds(1, 3)
    for cp in late:
        cp.wait()
    own_ng.wait()
    local(ux.at[0], ux.at[0], own_s.at[1]).wait()
    remote(ngx.at[others], ngx.at[others], dp_s.at[0], dp_r.at[0], mp=m).wait_recv()
    remote(hx.at[others], hx.at[others], dp_s.at[1], dp_r.at[1], mp=m).wait_recv()
    for k in range(4):
        ngt[:, pl.ds(ROWS * k, ROWS)] = ngx[k].T
    remote(ux.at[others], ux.at[others], dp_s.at[3], dp_r.at[3], mp=m).wait_recv()
    for k in range(4):
        uxt[:, pl.ds(ROWS * k, ROWS)] = ux[k].T

    def down_tile(j, carry):
        cols = pl.ds(pl.multiple_of(j * 256, 256), 256)
        hidden = hx[:, :, cols].reshape(4 * ROWS, 256)
        down_sum = dot_nn(uxt[...], hidden)
        new_first = 0.9 * fm[:, cols] + 0.1 * down_sum
        new_second = 0.95 * sm[:, cols] + 0.05 * down_sum * down_sum
        ad[:, cols] = new_first / first_fix / (jnp.sqrt(new_second / second_fix) + 1e-08)
        return carry

    lax.fori_loop(0, UNITS // 256, down_tile, 0)
    ad_out = local(ad, ad_o.at[0], out_s.at[0])
    ad_out.start()
    remote(gx.at[others], gx.at[others], dp_s.at[2], dp_r.at[2], mp=m).wait_recv()

    def grad_tile(j, carry):
        cols = pl.ds(pl.multiple_of(j * 256, 256), 256)
        cols_up = pl.ds(pl.multiple_of(UNITS + j * 256, 256), 256)
        gate = gx[:, :, cols].reshape(4 * ROWS, 256)
        gg[:, cols] = dot_nn(ngt[...], gate).astype(BF16)
        upg = gx[:, :, cols_up].reshape(4 * ROWS, 256)
        ug[:, cols] = dot_nn(ngt[...], upg).astype(BF16)
        return carry

    lax.fori_loop(0, UNITS // 256, grad_tile, 0)
    gg_out = local(gg, gg_o.at[0], out_s.at[1])
    ug_out = local(ug, ug_o.at[0], out_s.at[2])
    gg_out.start()
    ug_out.start()

    def last_chunk(c, carry):
        remote(igbuf.at[c], igbuf.at[c], rs_s.at[0], ig_r.at[c], mp=m).wait_recv()
        unpack(igbuf, c, ig)
        rows = pl.ds(pl.multiple_of(CH * c, CH), CH)
        local(ig.at[rows], ig_o.at[0, rows], out_s.at[3]).start()
        return carry

    lax.fori_loop(0, CHUNKS, last_chunk, 0)

    for cp in li_sends:
        cp.wait_send()
    gn_send.wait_send()
    remote(snd, snd, rs_s.at[0], rs_r.at[0, 0], mp=m).wait_send()
    remote(ngx.at[others], ngx.at[others], dp_s.at[0], dp_r.at[0], mp=m).wait_send()
    remote(hx.at[others], hx.at[others], dp_s.at[1], dp_r.at[1], mp=m).wait_send()
    remote(gx.at[others], gx.at[others], dp_s.at[2], dp_r.at[2], mp=m).wait_send()
    remote(ux.at[others], ux.at[others], dp_s.at[3], dp_r.at[3], mp=m).wait_send()

    @pl.when(s < 3)
    def _():
        remote(agbuf, agbuf, fw_s.at[0], ag_r.at[0], mp=m).wait_send()

    @pl.when(s == 0)
    def _():
        wait_gather_sends()
        for i in range(2):
            remote(rout.at[1, i], incb.at[i], inc_s.at[i], inc_r.at[i], mp=m).wait_send()

    @pl.when(s == 3)
    def _():
        wait_gather_sends()

    ad_out.wait()
    gg_out.wait()
    ug_out.wait()
    local(ig, ig_o.at[0], out_s.at[3]).wait()


def on_device(layer_input, top_grad, norm_gain, gate_weight, up_weight, down_weight, first_moment, second_moment):
    V, DMA = pltpu.VMEM, pltpu.SemaphoreType.DMA
    pieces = (16, HALF)
    return pl.pallas_call(
        kernel,
        out_shape=(
            jax.ShapeDtypeStruct((1, ROWS, D), BF16),
            jax.ShapeDtypeStruct((1, 512, UNITS), BF16),
            jax.ShapeDtypeStruct((1, 512, UNITS), BF16),
            jax.ShapeDtypeStruct((1, 512, UNITS), F32),
        ),
        in_specs=[pl.BlockSpec(memory_space=pl.ANY)] * 8,
        out_specs=[pl.BlockSpec(memory_space=pl.ANY)] * 4,
        scratch_shapes=[
            V((ROWS, D), BF16),
            V((D, 2 * UNITS), BF16),
            V((UNITS, D), BF16),
            V((ROWS, D), BF16),
            V((1, D), F32),
            V((512, UNITS), F32),
            V((512, UNITS), F32),
            V((ROWS, D), BF16),
            V((ROWS, UNITS), F32),
            V((ROWS, UNITS), F32),
            V((4, ROWS, 2 * UNITS), BF16),
            V((4, ROWS, UNITS), BF16),
            V((4, ROWS, 512), BF16),
            V((4, ROWS, 512), BF16),
            V((512, 4 * ROWS), BF16),
            V((512, 4 * ROWS), BF16),
            V((CHUNKS, BLOCKS) + pieces, BF16),
            V((2, 2, 16) + pieces, BF16),
            V((2, 2) + pieces, BF16),
            V((CHUNKS, BLOCKS) + pieces, BF16),
            V((CHUNKS, BLOCKS) + pieces, BF16),
            V((ROWS, D), BF16),
            V((512, UNITS), BF16),
            V((512, UNITS), BF16),
            V((512, UNITS), F32),
            V((2, 2, 16, D), BF16),
            V((2, 1, D), F32),
            V((2,) + pieces, BF16),
            V((2, 16, D), BF16),
            DMA((10,)),
            DMA((2, 2)),
            DMA((CHUNKS,)),
            DMA((CHUNKS,)),
            DMA((2, 2)),
            DMA((2,)),
            DMA((2,)),
            DMA((4,)),
            DMA((1,)),
            DMA((2, 2)),
            DMA((2,)),
            DMA((2,)),
            DMA((1,)),
            DMA((1,)),
            DMA((4,)),
            DMA((2,)),
            DMA((4,)),
        ],
        compiler_params=pltpu.CompilerParams(has_side_effects=True, vmem_limit_bytes=50 * 1024 * 1024),
        name="relay",
    )(layer_input, top_grad, norm_gain, gate_weight, up_weight, down_weight, first_moment, second_moment)


def solution(mesh):
    return jax.shard_map(
        on_device,
        mesh=mesh,
        in_specs=(
            P("section", "dp", None),
            P("dp", None),
            P("section", None),
            P("section", None, "mp"),
            P("section", None, "mp"),
            P("section", "mp", None),
            P("section", "dp", "mp"),
            P("section", "dp", "mp"),
        ),
        out_specs=(
            P("section", "dp", None),
            P("section", "dp", "mp"),
            P("section", "dp", "mp"),
            P("section", "dp", "mp"),
        ),
        check_vma=False,
    )
```

```python
import jax
import jax.numpy as jnp
from jax import lax
from jax.experimental import pallas as pl
from jax.experimental.pallas import tpu as pltpu
from jax.sharding import PartitionSpec as P

first_fix = 1.0 - 0.9**20
second_fix = 1.0 - 0.95**20

MESH = pl.DeviceIdType.MESH
F32 = jnp.float32
BF16 = jnp.bfloat16

ROWS = 256
D = 2048
UNITS = 512
QUARTER = D // 4
CHUNKS = 8
CH = ROWS // CHUNKS
BLOCKS = CH // 4
TURNS = CHUNKS // 2
FAR_FIRST = (4, 3, 5, 2, 6, 1, 7, 0)


def dot_nn(left, right):
    return lax.dot_general(left, right, (((1,), (0,)), ((), ())), preferred_element_type=F32)


def dot_nt(left, right):
    return lax.dot_general(left, right, (((1,), (1,)), ((), ())), preferred_element_type=F32)


def swap(a, b):
    low = lax.broadcasted_iota(jnp.int32, a.shape, 0) < 4
    first = jnp.where(low, a, pltpu.roll(b, 4, 0))
    second = jnp.where(low, pltpu.roll(a, 4, 0), b)
    return first, second


def pack(quarters):
    a_top, b_top = swap(quarters[0], quarters[1])
    a_low, b_low = swap(quarters[2], quarters[3])
    return jnp.concatenate([a_top, a_low], axis=0), jnp.concatenate([b_top, b_low], axis=0)


def unpack_pair(a, b):
    first = swap(a[:8], b[:8])
    second = swap(a[8:], b[8:])
    return first + second


def row_sums(packed):
    folded = packed[:8] + packed[8:]
    folded = folded + pltpu.roll(folded, 4, 0)
    sums = jnp.sum(folded, axis=-1, keepdims=True)
    return jnp.concatenate([sums, sums], axis=0)


def quarters_of(rows):
    return [rows[:, QUARTER * q : QUARTER * (q + 1)] for q in range(4)]


def kernel(
    li_h, tg_h, gain_h, gw_h, uw_h, dw_h, fm_h, sm_h,
    ig, gg, ug, ad,
    li, w, dw, wt, dwt, up, gain, fm, sm,
    ng, gated, slope, gx, hx, ngx, ux, ngt, uxt,
    snd, rsbuf, rout, agbuf, igbuf,
    lisend, liown, gnown, incb, tgown,
    ld, rs_r, ag_r, ig_r, li_r, gn_r, inc_r, dp_r,
    rs_s, ag_s, inc_s, li_s, gn_s, fw_s, dp_s, own_s,
):
    d = lax.axis_index("dp")
    s = lax.axis_index("section")
    m = lax.axis_index("mp")
    yh, z = m // 8, m % 8
    owner = jnp.where(s >= 2, 0, 3)
    turn = 1 - s % 2

    def local(src, dst, sem):
        return pltpu.make_async_copy(src, dst, sem)

    def remote(src, dst, ssem, rsem, **to):
        return pltpu.make_async_remote_copy(src, dst, ssem, rsem, device_id=to, device_id_type=MESH)

    li_load = local(li_h.at[0], li, ld.at[0])
    gain_load = local(gain_h, gain, ld.at[1])
    gw_load = local(gw_h.at[0], w.at[:, pl.ds(0, UNITS)], ld.at[2])
    uw_load = local(uw_h.at[0], w.at[:, pl.ds(UNITS, UNITS)], ld.at[3])
    dw_load = local(dw_h.at[0], dw, ld.at[4])
    late = [local(fm_h.at[0], fm, ld.at[5]), local(sm_h.at[0], sm, ld.at[6])]
    tg_load = local(tg_h, up, ld.at[7])

    def own_tile(i):
        return pl.ds(pl.multiple_of(CH * (yh + 2 * i) + 16 * (z // 4), 16), 16)

    tg_rows = [local(tg_h.at[own_tile(i)], tgown.at[i], ld.at[8 + i]) for i in range(TURNS)]

    li_load.start()
    gain_load.start()

    @pl.when(s == 3)
    def _():
        tg_load.start()

    gw_load.start()
    uw_load.start()
    dw_load.start()

    @pl.when(s == 0)
    def _():
        for cp in tg_rows:
            cp.start()

    for cp in late:
        cp.start()

    barrier = pltpu.get_barrier_semaphore()

    def greet(**to):
        pl.semaphore_signal(barrier, inc=1, device_id=to, device_id_type=MESH)

    def greet_all(section):
        def one(j, carry):
            greet(section=section, mp=j)
            return carry
        lax.fori_loop(0, 16, one, 0)

    for k in (1, 2, 3):
        greet(dp=lax.rem(d + k, 4))

    @pl.when(s == 3)
    def _():
        greet_all(0)
        greet_all(1)
        greet(section=2)

    @pl.when(s == 2)
    def _():
        greet_all(0)
        greet(section=1)

    @pl.when(s == 1)
    def _():
        greet_all(0)

    @pl.when(s == 0)
    def _():
        greet_all(3)
        greet_all(2)

    def own_piece(tile):
        tile = tile.astype(F32)
        rows = jnp.where((z // 2) % 2 == 0, tile[:8], tile[8:])
        a, b = pack(quarters_of(rows))
        return jnp.where(z % 2 == 0, a, b)

    li_load.wait()
    gain_load.wait()
    for i in range(TURNS):
        lisend[i] = own_piece(li[own_tile(i), :]).astype(BF16)
    li_send = remote(lisend, liown.at[turn], li_s.at[0], li_r.at[turn], section=owner)
    gn_send = remote(gain, gnown.at[turn], gn_s.at[0], gn_r.at[turn], section=owner)

    def norm_rows(j, carry):
        rows = pl.ds(pl.multiple_of(j * 32, 32), 32)
        values = li[rows, :].astype(F32)
        scale_inv = lax.rsqrt(jnp.mean(values * values, axis=-1, keepdims=True) + 1e-05)
        ng[rows, :] = (values * scale_inv * gain[...]).astype(BF16)
        return carry

    lax.fori_loop(0, ROWS // 32, norm_rows, 0)
    gw_load.wait()
    uw_load.wait()

    def forward(j, carry):
        cols = pl.ds(pl.multiple_of(j * 256, 256), 256)
        cols_up = pl.ds(pl.multiple_of(UNITS + j * 256, 256), 256)
        gate_pre = dot_nn(ng[...], w[:, cols])
        up_pre = dot_nn(ng[...], w[:, cols_up])
        sig = jax.nn.sigmoid(gate_pre)
        gate = gate_pre * sig
        gated[:, cols] = gate
        hx[0, :, cols] = (gate * up_pre).astype(BF16)
        slope[:, cols] = up_pre * sig * (1.0 + gate_pre * (1.0 - sig))
        return carry

    lax.fori_loop(0, UNITS // 256, forward, 0)

    @pl.when(s == 3)
    def _():
        pl.semaphore_wait(barrier, 19)

    @pl.when((s == 2) | (s == 1))
    def _():
        pl.semaphore_wait(barrier, 20)

    @pl.when(s == 0)
    def _():
        pl.semaphore_wait(barrier, 51)

    li_send.start()
    gn_send.start()
    dw_load.wait()

    def feature_cols(k):
        return pl.ds(pl.multiple_of(lax.rem(d + k, 4) * 512, 512), 512)

    own_ng = local(ng.at[:, feature_cols(0)], ngx.at[0], own_s.at[0])

    def bulk():
        own_ng.start()
        for k in (2, 1, 3):
            peer = lax.rem(d + k, 4)
            remote(ng.at[:, feature_cols(k)], ngx.at[4 - k], dp_s.at[0], dp_r.at[0], dp=peer).start()
            remote(hx.at[0], hx.at[4 - k], dp_s.at[1], dp_r.at[1], dp=peer).start()

    def reduce_layer(u, incoming, sends):
        def chunk(i, carry):
            remote(rsbuf.at[u, i], rsbuf.at[u, i], rs_s.at[0], rs_r.at[u, i], mp=m).wait_recv()
            values = liown[u, i].astype(F32)
            scale_inv = lax.rsqrt(row_sums(values * values) * (1.0 / D) + 1e-05)
            normed = values * scale_inv
            total = rsbuf[u, i, 0].astype(F32)
            for k in range(1, 16):
                total = total + rsbuf[u, i, k].astype(F32)
            quarter = lax.broadcasted_iota(jnp.int32, (16, QUARTER), 0) // 4
            gain_piece = jnp.zeros((16, QUARTER), F32)
            for q in range(4):
                gain_piece = jnp.where(quarter == q, gnown[u, :, pl.ds(QUARTER * q, QUARTER)], gain_piece)
            scaled = total * gain_piece
            projection = row_sums(scaled * normed) * (1.0 / D)
            rout[u, i] = (incoming(i) + scale_inv * (scaled - normed * projection)).astype(BF16)
            sends(u, i)
            return carry

        lax.fori_loop(0, TURNS, chunk, 0)

    def gather_to(section, buf, sem):
        def sends(u, i):
            chunk = yh + 2 * i
            for k in FAR_FIRST:
                for h in range(2):
                    to = lax.rem(z + k, 8) + 8 * h
                    remote(
                        rout.at[u, i], buf.at[chunk, z], ag_s.at[u], sem.at[chunk], section=section, mp=to
                    ).start()
        return sends

    def own_rows_ready(u):
        remote(liown.at[u], liown.at[u], li_s.at[0], li_r.at[u], mp=m).wait_recv()
        remote(gnown.at[u], gnown.at[u], gn_s.at[0], gn_r.at[u], mp=m).wait_recv()

    def from_rout(i):
        return rout[0, i].astype(F32)

    def wait_gather_sends():
        for u in range(2):
            remote(rsbuf.at[u], rsbuf.at[u], ag_s.at[u], rs_r.at[u, 0], mp=m).wait_send()

    @pl.when(s < 3)
    def _():
        bulk()

        def turn_w(j, carry):
            rows = pl.ds(pl.multiple_of(j * 256, 256), 256)
            wt[:, rows] = w[rows, :].T
            return carry

        lax.fori_loop(0, D // 256, turn_w, 0)

        def turn_dw(j, carry):
            rows = pl.ds(pl.multiple_of(j * 256, 256), 256)
            dwt[:, rows] = dw[rows, :].T
            return carry

        lax.fori_loop(0, UNITS // 256, turn_dw, 0)

    @pl.when(s == 0)
    def _():
        for cp in tg_rows:
            cp.wait()
        own_rows_ready(0)
        own_rows_ready(1)

        def from_top(i):
            return own_piece(tgown[i])

        def sends_two(u, i):
            gather_to(1, agbuf, ag_r)(u, i)
            remote(rout.at[u, i], incb.at[i], inc_s.at[0], inc_r.at[i], section=3).start()

        reduce_layer(0, from_top, gather_to(2, agbuf, ag_r))
        reduce_layer(1, from_rout, sends_two)

    below = jnp.where(s == 3, 0, s + 1)

    def unpack(src, c, dst):
        for p in range(2):
            rows = pl.ds(pl.multiple_of(CH * c + 16 * p, 16), 16)
            top = unpack_pair(src[c, 4 * p].astype(F32), src[c, 4 * p + 1].astype(F32))
            low = unpack_pair(src[c, 4 * p + 2].astype(F32), src[c, 4 * p + 3].astype(F32))
            for q in range(4):
                both = jnp.concatenate([top[q], low[q]], axis=0)
                dst[rows, pl.ds(QUARTER * q, QUARTER)] = both.astype(BF16)

    def send_partials(c, product):
        for t in range(2):
            quarters = [product(QUARTER * q + 256 * t) for q in range(4)]
            cols = pl.ds(256 * t, 256)
            for b in range(BLOCKS // 2):
                first, second = pack([x[8 * b : 8 * b + 8] for x in quarters])
                snd[c, 2 * b, :, cols] = first.astype(BF16)
                snd[c, 2 * b + 1, :, cols] = second.astype(BF16)
        for k in FAR_FIRST:
            to = lax.rem(z + k, 8)
            remote(
                snd.at[c, to], rsbuf.at[turn, c // 2, m], rs_s.at[0], rs_r.at[turn, c // 2],
                section=owner, mp=to + 8 * (c % 2),
            ).start()

    def share(start, size):
        rows = pl.ds(pl.multiple_of(start, CH), size)
        local(up.at[rows, feature_cols(0)], ux.at[0, rows], own_s.at[1]).start()
        for k in (2, 1, 3):
            peer = lax.rem(d + k, 4)
            remote(gx.at[0, rows], gx.at[4 - k, rows], dp_s.at[2], dp_r.at[2], dp=peer).start()
            remote(up.at[rows, feature_cols(k)], ux.at[4 - k, rows], dp_s.at[3], dp_r.at[3], dp=peer).start()

    @pl.when(s == 3)
    def _():
        tg_load.wait()

        def hidden_tile(j, carry):
            cols = pl.ds(pl.multiple_of(j * 256, 256), 256)
            cols_up = pl.ds(pl.multiple_of(UNITS + j * 256, 256), 256)
            grad_hidden = dot_nt(up[...], dw[cols, :])
            gx[0, :, cols] = (grad_hidden * slope[:, cols]).astype(BF16)
            gx[0, :, cols_up] = (grad_hidden * gated[:, cols]).astype(BF16)
            return carry

        lax.fori_loop(0, UNITS // 256, hidden_tile, 0)

        def chunk_step(c, carry):
            rows = pl.ds(pl.multiple_of(CH * c, CH), CH)
            send_partials(c, lambda at: dot_nt(gx[0, rows, :], w[pl.ds(at, 256), :]))
            return carry

        lax.fori_loop(0, CHUNKS, chunk_step, 0)
        bulk()
        share(0, ROWS)

    @pl.when(s < 3)
    def _():
        def chunk_step(c, carry):
            rows = pl.ds(pl.multiple_of(CH * c, CH), CH)
            remote(agbuf.at[c], agbuf.at[c], rs_s.at[0], ag_r.at[c], mp=m).wait_recv()
            unpack(agbuf, c, up)
            grad_hidden = dot_nn(up[rows, :], dwt[...])
            gx[0, rows, pl.ds(0, UNITS)] = (grad_hidden * slope[rows, :]).astype(BF16)
            gx[0, rows, pl.ds(UNITS, UNITS)] = (grad_hidden * gated[rows, :]).astype(BF16)
            send_partials(c, lambda at: dot_nn(gx[0, rows, :], wt[:, pl.ds(at, 256)]))

            @pl.when(s == 0)
            def _():
                share(CH * c, CH)

            @pl.when((s > 0) & (c % 4 == 3))
            def _():
                share((c // 4) * 128, 128)

            @pl.when(c % 4 == 3)
            def _():
                half = pl.ds(pl.multiple_of((c // 4) * 4, 4), 4)
                remote(agbuf.at[half], igbuf.at[half], fw_s.at[0], ig_r.at[c // 4], section=below).start()

            return carry

        lax.fori_loop(0, CHUNKS, chunk_step, 0)

    @pl.when(s == 3)
    def _():
        own_rows_ready(0)
        own_rows_ready(1)

        def from_inc(i):
            remote(incb.at[i], incb.at[i], inc_s.at[0], inc_r.at[i], mp=m).wait_recv()
            return incb[i].astype(F32)

        reduce_layer(0, from_inc, gather_to(0, agbuf, ag_r))
        reduce_layer(1, from_rout, gather_to(0, igbuf, ig_r))

    others = pl.ds(1, 3)
    for cp in late:
        cp.wait()
    own_ng.wait()
    local(ux.at[0], ux.at[0], own_s.at[1]).wait()
    remote(ngx.at[others], ngx.at[others], dp_s.at[0], dp_r.at[0], mp=m).wait_recv()
    remote(hx.at[others], hx.at[others], dp_s.at[1], dp_r.at[1], mp=m).wait_recv()
    for k in range(4):
        ngt[:, pl.ds(ROWS * k, ROWS)] = ngx[k].T
    remote(ux.at[others], ux.at[others], dp_s.at[3], dp_r.at[3], mp=m).wait_recv()
    for k in range(4):
        uxt[:, pl.ds(ROWS * k, ROWS)] = ux[k].T

    def down_tile(j, carry):
        cols = pl.ds(pl.multiple_of(j * 256, 256), 256)
        hidden = hx[:, :, cols].reshape(4 * ROWS, 256)
        down_sum = dot_nn(uxt[...], hidden)
        new_first = 0.9 * fm[:, cols] + 0.1 * down_sum
        new_second = 0.95 * sm[:, cols] + 0.05 * down_sum * down_sum
        ad[0, :, cols] = new_first / first_fix / (jnp.sqrt(new_second / second_fix) + 1e-08)
        return carry

    lax.fori_loop(0, UNITS // 256, down_tile, 0)
    remote(gx.at[others], gx.at[others], dp_s.at[2], dp_r.at[2], mp=m).wait_recv()

    def grad_tile(j, carry):
        cols = pl.ds(pl.multiple_of(j * 256, 256), 256)
        cols_up = pl.ds(pl.multiple_of(UNITS + j * 256, 256), 256)
        gate = gx[:, :, cols].reshape(4 * ROWS, 256)
        gg[0, :, cols] = dot_nn(ngt[...], gate).astype(BF16)
        upg = gx[:, :, cols_up].reshape(4 * ROWS, 256)
        ug[0, :, cols] = dot_nn(ngt[...], upg).astype(BF16)
        return carry

    lax.fori_loop(0, UNITS // 256, grad_tile, 0)

    @pl.when(s > 0)
    def _():
        for h in range(2):
            half = pl.ds(4 * h, 4)
            remote(igbuf.at[half], igbuf.at[half], rs_s.at[0], ig_r.at[h], mp=m).wait_recv()

    def last_chunk(c, carry):
        @pl.when(s == 0)
        def _():
            remote(igbuf.at[c], igbuf.at[c], rs_s.at[0], ig_r.at[c], mp=m).wait_recv()

        unpack(igbuf, c, ig.at[0])
        return carry

    lax.fori_loop(0, CHUNKS, last_chunk, 0)

    li_send.wait_send()
    gn_send.wait_send()
    remote(snd, snd, rs_s.at[0], rs_r.at[0, 0], mp=m).wait_send()
    remote(ngx.at[others], ngx.at[others], dp_s.at[0], dp_r.at[0], mp=m).wait_send()
    remote(hx.at[others], hx.at[others], dp_s.at[1], dp_r.at[1], mp=m).wait_send()
    remote(gx.at[others], gx.at[others], dp_s.at[2], dp_r.at[2], mp=m).wait_send()
    remote(ux.at[others], ux.at[others], dp_s.at[3], dp_r.at[3], mp=m).wait_send()

    @pl.when(s < 3)
    def _():
        remote(agbuf, agbuf, fw_s.at[0], ag_r.at[0], mp=m).wait_send()

    @pl.when(s == 0)
    def _():
        wait_gather_sends()
        remote(rout.at[1], incb, inc_s.at[0], inc_r.at[0], mp=m).wait_send()

    @pl.when(s == 3)
    def _():
        wait_gather_sends()


def hand_on(*refs):
    sources, targets, sems = refs[:4], refs[4:8], refs[8]
    copies = [pltpu.make_async_copy(a, b, sems.at[i]) for i, (a, b) in enumerate(zip(sources, targets))]
    for cp in copies:
        cp.start()
    for cp in copies:
        cp.wait()


def on_device(layer_input, top_grad, norm_gain, gate_weight, up_weight, down_weight, first_moment, second_moment):
    V, DMA = pltpu.VMEM, pltpu.SemaphoreType.DMA
    pieces = (16, QUARTER)
    shapes = (
        jax.ShapeDtypeStruct((1, ROWS, D), BF16),
        jax.ShapeDtypeStruct((1, 512, UNITS), BF16),
        jax.ShapeDtypeStruct((1, 512, UNITS), BF16),
        jax.ShapeDtypeStruct((1, 512, UNITS), F32),
    )
    norm_gain = pltpu.with_memory_space_constraint(norm_gain, pltpu.HBM)
    results = pl.pallas_call(
        kernel,
        out_shape=shapes,
        in_specs=[pl.BlockSpec(memory_space=pltpu.HBM)] * 8,
        out_specs=[pl.BlockSpec(memory_space=pltpu.VMEM)] * 4,
        scratch_shapes=[
            V((ROWS, D), BF16),
            V((D, 2 * UNITS), BF16),
            V((UNITS, D), BF16),
            V((2 * UNITS, D), BF16),
            V((D, UNITS), BF16),
            V((ROWS, D), BF16),
            V((1, D), F32),
            V((512, UNITS), F32),
            V((512, UNITS), F32),
            V((ROWS, D), BF16),
            V((ROWS, UNITS), F32),
            V((ROWS, UNITS), F32),
            V((4, ROWS, 2 * UNITS), BF16),
            V((4, ROWS, UNITS), BF16),
            V((4, ROWS, 512), BF16),
            V((4, ROWS, 512), BF16),
            V((512, 4 * ROWS), BF16),
            V((512, 4 * ROWS), BF16),
            V((CHUNKS, BLOCKS) + pieces, BF16),
            V((2, TURNS, 16) + pieces, BF16),
            V((2, TURNS) + pieces, BF16),
            V((CHUNKS, BLOCKS) + pieces, BF16),
            V((CHUNKS, BLOCKS) + pieces, BF16),
            V((TURNS,) + pieces, BF16),
            V((2, TURNS) + pieces, BF16),
            V((2, 1, D), F32),
            V((TURNS,) + pieces, BF16),
            V((TURNS, 16, D), BF16),
            DMA((8 + TURNS,)),
            DMA((2, TURNS)),
            DMA((CHUNKS,)),
            DMA((CHUNKS,)),
            DMA((2,)),
            DMA((2,)),
            DMA((TURNS,)),
            DMA((4,)),
            DMA((1,)),
            DMA((2,)),
            DMA((1,)),
            DMA((1,)),
            DMA((1,)),
            DMA((1,)),
            DMA((4,)),
            DMA((2,)),
        ],
        compiler_params=pltpu.CompilerParams(
            has_side_effects=True, collective_id=0, vmem_limit_bytes=50 * 1024 * 1024
        ),
        name="relay",
    )(layer_input, top_grad, norm_gain, gate_weight, up_weight, down_weight, first_moment, second_moment)
    return pl.pallas_call(
        hand_on,
        out_shape=shapes,
        in_specs=[pl.BlockSpec(memory_space=pltpu.VMEM)] * 4,
        out_specs=[pl.BlockSpec(memory_space=pltpu.HBM)] * 4,
        scratch_shapes=[DMA((4,))],
        compiler_params=pltpu.CompilerParams(vmem_limit_bytes=8 * 1024 * 1024),
        name="hand_on",
    )(*results)


def solution(mesh):
    return jax.shard_map(
        on_device,
        mesh=mesh,
        in_specs=(
            P("section", "dp", None),
            P("dp", None),
            P("section", None),
            P("section", None, "mp"),
            P("section", None, "mp"),
            P("section", "mp", None),
            P("section", "dp", "mp"),
            P("section", "dp", "mp"),
        ),
        out_specs=(
            P("section", "dp", None),
            P("section", "dp", "mp"),
            P("section", "dp", "mp"),
            P("section", "dp", "mp"),
        ),
        check_vma=False,
    )
```

```python
import jax
import jax.numpy as jnp
from jax import lax
from jax.experimental import pallas as pl
from jax.experimental.pallas import tpu as pltpu
from jax.sharding import PartitionSpec as P

first_fix = 1.0 - 0.9**20
second_fix = 1.0 - 0.95**20

MESH = pl.DeviceIdType.MESH
F32 = jnp.float32
BF16 = jnp.bfloat16

ROWS = 256
D = 2048
UNITS = 512
QUARTER = D // 4
CHUNKS = 8
CH = ROWS // CHUNKS
BLOCKS = CH // 4
TURNS = CHUNKS // 2
EARLY = 4
FAR_FIRST = (4, 3, 5, 2, 6, 1, 7, 0)


def dot_nn(left, right):
    return lax.dot_general(left, right, (((1,), (0,)), ((), ())), preferred_element_type=F32)


def dot_nt(left, right):
    return lax.dot_general(left, right, (((1,), (1,)), ((), ())), preferred_element_type=F32)


def swap(a, b):
    low = lax.broadcasted_iota(jnp.int32, a.shape, 0) < 4
    first = jnp.where(low, a, pltpu.roll(b, 4, 0))
    second = jnp.where(low, pltpu.roll(a, 4, 0), b)
    return first, second


def pack(quarters):
    a_top, b_top = swap(quarters[0], quarters[1])
    a_low, b_low = swap(quarters[2], quarters[3])
    return jnp.concatenate([a_top, a_low], axis=0), jnp.concatenate([b_top, b_low], axis=0)


def unpack_pair(a, b):
    first = swap(a[:8], b[:8])
    second = swap(a[8:], b[8:])
    return first + second


def row_sums(packed):
    folded = packed[:8] + packed[8:]
    folded = folded + pltpu.roll(folded, 4, 0)
    sums = jnp.sum(folded, axis=-1, keepdims=True)
    return jnp.concatenate([sums, sums], axis=0)


def quarters_of(rows):
    return [rows[:, QUARTER * q : QUARTER * (q + 1)] for q in range(4)]


def kernel(
    li_h, tg_h, gain_h, gw_h, uw_h, dw_h, fm_h, sm_h,
    ig, gg, ug, ad,
    li, w, dw, wt, dwt, up, gain, fm, sm,
    ng, gated, slope, gh, gx, hx, ngx, ux, ngt, uxt, acc,
    snd, rsbuf, rs2, rout, rout2, agbuf, igbuf,
    lisend, liown, liown2, gnown, gnown2, incb, inc2, tgown,
    ld, rs_r, rs2_r, ag_r, ig_r, li_r, gn_r, inc_r, inc2_r, dp_r,
    rs_s, ag_s, inc_s, li_s, gn_s, fw_s, dp_s, own_s,
):
    d = lax.axis_index("dp")
    s = lax.axis_index("section")
    m = lax.axis_index("mp")
    yh, z = m // 8, m % 8
    owner = jnp.where(s >= 2, 0, 3)
    turn = 1 - s % 2

    def local(src, dst, sem):
        return pltpu.make_async_copy(src, dst, sem)

    def remote(src, dst, ssem, rsem, **to):
        return pltpu.make_async_remote_copy(src, dst, ssem, rsem, device_id=to, device_id_type=MESH)

    li_load = local(li_h.at[0], li, ld.at[0])
    gain_load = local(gain_h, gain, ld.at[1])
    gw_load = local(gw_h.at[0], w.at[:, pl.ds(0, UNITS)], ld.at[2])
    uw_load = local(uw_h.at[0], w.at[:, pl.ds(UNITS, UNITS)], ld.at[3])
    dw_load = local(dw_h.at[0], dw, ld.at[4])
    late = [local(fm_h.at[0], fm, ld.at[5]), local(sm_h.at[0], sm, ld.at[6])]
    tg_load = local(tg_h, up, ld.at[7])

    def own_tile(i):
        return pl.ds(pl.multiple_of(CH * (yh + 2 * i) + 16 * (z // 4), 16), 16)

    tg_rows = [local(tg_h.at[own_tile(i)], tgown.at[i], ld.at[8 + i]) for i in range(TURNS)]

    barrier = pltpu.get_barrier_semaphore()

    def greet(**to):
        pl.semaphore_signal(barrier, inc=1, device_id=to, device_id_type=MESH)

    def greet_all(section):
        def one(j, carry):
            greet(section=section, mp=j)
            return carry
        lax.fori_loop(0, 16, one, 0)

    @pl.when(s == 3)
    def _():
        greet_all(0)
        greet_all(1)
        greet_all(2)

    @pl.when(s == 2)
    def _():
        greet_all(0)
        greet(section=1)

    @pl.when(s == 1)
    def _():
        greet_all(0)
        greet_all(3)

    @pl.when(s == 0)
    def _():
        greet_all(3)
        greet_all(2)

    for k in (1, 2, 3):
        greet(dp=lax.rem(d + k, 4))

    li_load.start()
    gain_load.start()

    @pl.when(s == 3)
    def _():
        tg_load.start()

    dw_load.start()
    gw_load.start()
    uw_load.start()

    @pl.when(s == 0)
    def _():
        for cp in tg_rows:
            cp.start()

    for cp in late:
        cp.start()

    early, later = pl.ds(0, 2), pl.ds(2, 2)

    def own_piece(tile):
        tile = tile.astype(F32)
        rows = jnp.where((z // 2) % 2 == 0, tile[:8], tile[8:])
        a, b = pack(quarters_of(rows))
        return jnp.where(z % 2 == 0, a, b)

    li_load.wait()
    gain_load.wait()
    li_send = remote(lisend, liown.at[turn], li_s.at[0], li_r.at[turn], section=owner)
    gn_send = remote(gain, gnown.at[turn], gn_s.at[0], gn_r.at[turn], section=owner)

    def norm_rows(j, carry):
        rows = pl.ds(pl.multiple_of(j * 32, 32), 32)
        values = li[rows, :].astype(F32)
        scale_inv = lax.rsqrt(jnp.mean(values * values, axis=-1, keepdims=True) + 1e-05)
        ng[rows, :] = (values * scale_inv * gain[...]).astype(BF16)
        return carry

    lax.fori_loop(0, ROWS // 32, norm_rows, 0)
    dw_load.wait()

    @pl.when(s == 3)
    def _():
        tg_load.wait()

        def hidden_tile(j, carry):
            cols = pl.ds(pl.multiple_of(j * 256, 256), 256)
            gh[:, cols] = dot_nt(up[...], dw[cols, :])
            return carry

        lax.fori_loop(0, UNITS // 256, hidden_tile, 0)

    for i in range(TURNS):
        lisend[i] = own_piece(li[own_tile(i), :]).astype(BF16)

    gw_load.wait()
    uw_load.wait()

    def forward(j, carry):
        cols = pl.ds(pl.multiple_of(j * 256, 256), 256)
        cols_up = pl.ds(pl.multiple_of(UNITS + j * 256, 256), 256)
        gate_pre = dot_nn(ng[...], w[:, cols])
        up_pre = dot_nn(ng[...], w[:, cols_up])
        sig = jax.nn.sigmoid(gate_pre)
        gate = gate_pre * sig
        gated[:, cols] = gate
        hx[0, :, cols] = (gate * up_pre).astype(BF16)
        slope[:, cols] = up_pre * sig * (1.0 + gate_pre * (1.0 - sig))
        return carry

    lax.fori_loop(0, UNITS // 256, forward, 0)

    @pl.when(s >= 2)
    def _():
        pl.semaphore_wait(barrier, 35)

    @pl.when(s == 1)
    def _():
        pl.semaphore_wait(barrier, 20)

    @pl.when(s == 0)
    def _():
        pl.semaphore_wait(barrier, 51)

    li_send.start()
    gn_send.start()
    li_later = remote(lisend.at[later], liown2, li_s.at[1], li_r.at[2], section=3)
    gn_later = remote(gain, gnown2, gn_s.at[1], gn_r.at[2], section=3)

    @pl.when(s == 2)
    def _():
        li_later.start()
        gn_later.start()

    def feature_cols(k):
        return pl.ds(pl.multiple_of(lax.rem(d + k, 4) * 512, 512), 512)

    own_ng = local(ng.at[:, feature_cols(0)], ngx.at[0], own_s.at[0])

    def bulk():
        own_ng.start()
        for k in (2, 1, 3):
            peer = lax.rem(d + k, 4)
            remote(ng.at[:, feature_cols(k)], ngx.at[4 - k], dp_s.at[0], dp_r.at[0], dp=peer).start()
            remote(hx.at[0], hx.at[4 - k], dp_s.at[1], dp_r.at[1], dp=peer).start()

    def reduce_layer(buf, sem, own_rows, own_gain, out, incoming, sends, first, stop):
        def chunk(i, carry):
            remote(buf.at[i], buf.at[i], rs_s.at[0], sem.at[i], mp=m).wait_recv()
            values = own_rows[i].astype(F32)
            scale_inv = lax.rsqrt(row_sums(values * values) * (1.0 / D) + 1e-05)
            normed = values * scale_inv
            total = buf[i, 0].astype(F32)
            for k in range(1, 16):
                total = total + buf[i, k].astype(F32)
            quarter = lax.broadcasted_iota(jnp.int32, (16, QUARTER), 0) // 4
            gain_piece = jnp.zeros((16, QUARTER), F32)
            for q in range(4):
                gain_piece = jnp.where(quarter == q, own_gain[:, pl.ds(QUARTER * q, QUARTER)], gain_piece)
            scaled = total * gain_piece
            projection = row_sums(scaled * normed) * (1.0 / D)
            out[i] = (incoming(i) + scale_inv * (scaled - normed * projection)).astype(BF16)
            sends(i)
            return carry

        lax.fori_loop(first, stop, chunk, 0)

    def reduce_turn(u, incoming, sends, first, stop):
        reduce_layer(
            rsbuf.at[u], rs_r.at[u], liown.at[u], gnown.at[u], rout.at[u], incoming, sends, first, stop
        )

    def gather_to(section, buf, sem, out, ssem, base=0):
        def sends(i):
            chunk = yh + 2 * (i + base)
            for k in FAR_FIRST:
                for h in range(2):
                    to = lax.rem(z + k, 8) + 8 * h
                    remote(out.at[i], buf.at[chunk, z], ssem, sem.at[chunk], section=section, mp=to).start()
        return sends

    def own_rows_ready(u):
        remote(liown.at[u], liown.at[u], li_s.at[0], li_r.at[u], mp=m).wait_recv()
        remote(gnown.at[u], gnown.at[u], gn_s.at[0], gn_r.at[u], mp=m).wait_recv()

    def from_rout(i):
        return rout[0, i].astype(F32)

    others = pl.ds(1, 3)

    def turn_ng():
        own_ng.wait()
        remote(ngx.at[others], ngx.at[others], dp_s.at[0], dp_r.at[0], mp=m).wait_recv()
        for h in range(2):
            for k in range(4):
                ngt[h, :, pl.ds(128 * k, 128)] = ngx[k, pl.ds(128 * h, 128), :].T

    @pl.when(s < 3)
    def _():
        bulk()

        def turn_w(j, carry):
            rows = pl.ds(pl.multiple_of(j * 256, 256), 256)
            wt[:, rows] = w[rows, :].T
            return carry

        lax.fori_loop(0, D // 256, turn_w, 0)

        def turn_dw(j, carry):
            rows = pl.ds(pl.multiple_of(j * 256, 256), 256)
            dwt[:, rows] = dw[rows, :].T
            return carry

        lax.fori_loop(0, UNITS // 256, turn_dw, 0)

    @pl.when(s == 0)
    def _():
        for cp in tg_rows:
            cp.wait()
        own_rows_ready(0)
        own_rows_ready(1)

        def from_top(i):
            return own_piece(tgown[i])

        to_two = gather_to(2, agbuf, ag_r, rout.at[0], ag_s.at[0])
        to_one = gather_to(1, agbuf, ag_r, rout.at[1], ag_s.at[1])

        def sends_three(i):
            to_two(i)

            @pl.when(i >= 2)
            def _():
                remote(rout.at[0, i], inc2.at[i % 2], inc_s.at[1], inc2_r.at[i % 2], section=3).start()

        def sends_two(i):
            to_one(i)
            remote(rout.at[1, i], incb.at[i], inc_s.at[0], inc_r.at[i], section=3).start()

        reduce_turn(0, from_top, sends_three, 0, TURNS)
        reduce_turn(1, from_rout, sends_two, 0, 2)
        turn_ng()

    below = jnp.where(s == 3, 0, s + 1)

    def unpack(src, c, dst):
        for p in range(2):
            rows = pl.ds(pl.multiple_of(CH * c + 16 * p, 16), 16)
            top = unpack_pair(src[c, 4 * p].astype(F32), src[c, 4 * p + 1].astype(F32))
            low = unpack_pair(src[c, 4 * p + 2].astype(F32), src[c, 4 * p + 3].astype(F32))
            for q in range(4):
                both = jnp.concatenate([top[q], low[q]], axis=0)
                dst[rows, pl.ds(QUARTER * q, QUARTER)] = both.astype(BF16)

    def send_partials(c, product):
        for t in range(2):
            quarters = [product(QUARTER * q + 256 * t) for q in range(4)]
            cols = pl.ds(256 * t, 256)
            for b in range(BLOCKS // 2):
                first, second = pack([x[8 * b : 8 * b + 8] for x in quarters])
                snd[c, 2 * b, :, cols] = first.astype(BF16)
                snd[c, 2 * b + 1, :, cols] = second.astype(BF16)

        moved = (s == 2) & (c >= 4)

        @pl.when(moved)
        def _():
            for k in FAR_FIRST:
                to = lax.rem(z + k, 8)
                remote(
                    snd.at[c, to], rs2.at[(c // 2) % 2, m], rs_s.at[0], rs2_r.at[(c // 2) % 2],
                    section=3, mp=to + 8 * (c % 2),
                ).start()

        @pl.when(jnp.logical_not(moved))
        def _():
            for k in FAR_FIRST:
                to = lax.rem(z + k, 8)
                remote(
                    snd.at[c, to], rsbuf.at[turn, c // 2, m], rs_s.at[0], rs_r.at[turn, c // 2],
                    section=owner, mp=to + 8 * (c % 2),
                ).start()

    def share(start, size):
        rows = pl.ds(pl.multiple_of(start, CH), size)
        half = start // 128
        local(up.at[rows, feature_cols(0)], ux.at[0, rows], own_s.at[1 + half]).start()
        for k in (2, 1, 3):
            peer = lax.rem(d + k, 4)
            remote(gx.at[0, rows], gx.at[4 - k, rows], dp_s.at[2], dp_r.at[2 + half], dp=peer).start()
            remote(up.at[rows, feature_cols(k)], ux.at[4 - k, rows], dp_s.at[3], dp_r.at[4 + half], dp=peer).start()

    @pl.when(s == 3)
    def _():
        gx[0, :, pl.ds(0, UNITS)] = (gh[...] * slope[...]).astype(BF16)
        gx[0, :, pl.ds(UNITS, UNITS)] = (gh[...] * gated[...]).astype(BF16)

        def chunk_step(c, carry):
            rows = pl.ds(pl.multiple_of(CH * c, CH), CH)
            send_partials(c, lambda at: dot_nt(gx[0, rows, :], w[pl.ds(at, 256), :]))
            return carry

        lax.fori_loop(0, CHUNKS, chunk_step, 0)
        bulk()
        share(0, 128)
        share(128, 128)

    @pl.when(s < 3)
    def _():
        def chunk_step(c, carry):
            rows = pl.ds(pl.multiple_of(CH * c, CH), CH)
            remote(agbuf.at[c], agbuf.at[c], rs_s.at[0], ag_r.at[c], mp=m).wait_recv()
            unpack(agbuf, c, up)
            grad_hidden = dot_nn(up[rows, :], dwt[...])
            gx[0, rows, pl.ds(0, UNITS)] = (grad_hidden * slope[rows, :]).astype(BF16)
            gx[0, rows, pl.ds(UNITS, UNITS)] = (grad_hidden * gated[rows, :]).astype(BF16)
            send_partials(c, lambda at: dot_nn(gx[0, rows, :], wt[:, pl.ds(at, 256)]))

            @pl.when(s == 0)
            def _():
                share(CH * c, CH)

            @pl.when((s > 0) & (c % 4 == 3))
            def _():
                share((c // 4) * 128, 128)

            @pl.when(c % 4 == 3)
            def _():
                half = pl.ds(pl.multiple_of((c // 4) * 4, 4), 4)
                remote(agbuf.at[half], igbuf.at[half], fw_s.at[0], ig_r.at[c // 4], section=below).start()

            return carry

        lax.fori_loop(0, CHUNKS, chunk_step, 0)

    @pl.when(s == 3)
    def _():
        own_rows_ready(0)
        own_rows_ready(1)
        remote(liown2, liown2, li_s.at[0], li_r.at[2], mp=m).wait_recv()
        remote(gnown2, gnown2, gn_s.at[0], gn_r.at[2], mp=m).wait_recv()

        def from_above(i):
            remote(inc2.at[i], inc2.at[i], inc_s.at[0], inc2_r.at[i], mp=m).wait_recv()
            return inc2[i].astype(F32)

        def from_inc(i):
            remote(incb.at[i], incb.at[i], inc_s.at[0], inc_r.at[i], mp=m).wait_recv()
            return incb[i].astype(F32)

        def from_later(i):
            return rout2[i % 2].astype(F32)

        to_one = gather_to(1, agbuf, ag_r, rout2, ag_s.at[2], 2)
        reduce_layer(rs2, rs2_r, liown2, gnown2, rout2, from_above, to_one, 0, 2)
        to_zero = gather_to(0, agbuf, ag_r, rout.at[0], ag_s.at[0])
        reduce_turn(0, from_inc, to_zero, 0, 2)
        reduce_turn(0, from_later, to_zero, 2, TURNS)
        reduce_turn(1, from_rout, gather_to(0, igbuf, ig_r, rout.at[1], ag_s.at[1]), 0, TURNS)

    for cp in late:
        cp.wait()

    @pl.when(s > 0)
    def _():
        turn_ng()

    remote(hx.at[others], hx.at[others], dp_s.at[1], dp_r.at[1], mp=m).wait_recv()

    def last_chunk(c, carry):
        @pl.when(s == 0)
        def _():
            remote(igbuf.at[c], igbuf.at[c], rs_s.at[0], ig_r.at[c], mp=m).wait_recv()

        unpack(igbuf, c, ig.at[0])
        return carry

    for h in range(2):
        rows = pl.ds(128 * h, 128)
        local(ux.at[0, rows], ux.at[0, rows], own_s.at[1 + h]).wait()
        remote(ux.at[others, rows], ux.at[others, rows], dp_s.at[3], dp_r.at[4 + h], mp=m).wait_recv()
        for k in range(4):
            uxt[h, :, pl.ds(128 * k, 128)] = ux[k, rows, :].T
        remote(gx.at[others, rows], gx.at[others, rows], dp_s.at[2], dp_r.at[2 + h], mp=m).wait_recv()

        def grad_tile(j, carry):
            cols = pl.ds(pl.multiple_of(j * 256, 256), 256)
            cols_up = pl.ds(pl.multiple_of(UNITS + j * 256, 256), 256)
            down_sum = dot_nn(uxt[h], hx[:, rows, cols].reshape(2 * ROWS, 256))
            gate_sum = dot_nn(ngt[h], gx[:, rows, cols].reshape(2 * ROWS, 256))
            up_sum = dot_nn(ngt[h], gx[:, rows, cols_up].reshape(2 * ROWS, 256))
            if h == 0:
                acc[0, :, cols] = down_sum
                acc[1, :, cols] = gate_sum
                acc[2, :, cols] = up_sum
            else:
                down_sum = down_sum + acc[0, :, cols]
                gg[0, :, cols] = (gate_sum + acc[1, :, cols]).astype(BF16)
                ug[0, :, cols] = (up_sum + acc[2, :, cols]).astype(BF16)
                new_first = 0.9 * fm[:, cols] + 0.1 * down_sum
                new_second = 0.95 * sm[:, cols] + 0.05 * down_sum * down_sum
                ad[0, :, cols] = new_first / first_fix / (jnp.sqrt(new_second / second_fix) + 1e-08)
            return carry

        lax.fori_loop(0, UNITS // 256, grad_tile, 0)

        if h == 0:
            @pl.when(s == 0)
            def _():
                lax.fori_loop(0, EARLY, last_chunk, 0)

    @pl.when(s > 0)
    def _():
        for h in range(2):
            half = pl.ds(4 * h, 4)
            remote(igbuf.at[half], igbuf.at[half], rs_s.at[0], ig_r.at[h], mp=m).wait_recv()

    @pl.when(s > 0)
    def _():
        lax.fori_loop(0, EARLY, last_chunk, 0)

    lax.fori_loop(EARLY, CHUNKS, last_chunk, 0)

    li_send.wait_send()
    gn_send.wait_send()
    remote(snd, snd, rs_s.at[0], rs_r.at[0, 0], mp=m).wait_send()
    remote(ngx.at[others], ngx.at[others], dp_s.at[0], dp_r.at[0], mp=m).wait_send()
    remote(hx.at[others], hx.at[others], dp_s.at[1], dp_r.at[1], mp=m).wait_send()
    remote(gx.at[others], gx.at[others], dp_s.at[2], dp_r.at[2], mp=m).wait_send()
    remote(ux.at[others], ux.at[others], dp_s.at[3], dp_r.at[3], mp=m).wait_send()

    @pl.when(s < 3)
    def _():
        remote(agbuf, agbuf, fw_s.at[0], ag_r.at[0], mp=m).wait_send()

    @pl.when(s == 2)
    def _():
        li_later.wait_send()
        gn_later.wait_send()

    @pl.when(s == 0)
    def _():
        remote(rsbuf.at[0], rsbuf.at[0], ag_s.at[0], rs_r.at[0, 0], mp=m).wait_send()
        remote(rsbuf.at[1, early], rsbuf.at[1, early], ag_s.at[1], rs_r.at[0, 0], mp=m).wait_send()
        remote(rout.at[1, early], incb, inc_s.at[0], inc_r.at[0], mp=m).wait_send()
        remote(rout.at[0, later], inc2, inc_s.at[1], inc_r.at[0], mp=m).wait_send()

    @pl.when(s == 3)
    def _():
        for u in range(2):
            remote(rsbuf.at[u], rsbuf.at[u], ag_s.at[u], rs_r.at[0, 0], mp=m).wait_send()
        remote(rs2, rs2, ag_s.at[2], rs_r.at[0, 0], mp=m).wait_send()


def hand_on(*refs):
    sources, targets, sems = refs[:4], refs[4:8], refs[8]
    copies = [pltpu.make_async_copy(a, b, sems.at[i]) for i, (a, b) in enumerate(zip(sources, targets))]
    for cp in copies:
        cp.start()
    for cp in copies:
        cp.wait()


def on_device(layer_input, top_grad, norm_gain, gate_weight, up_weight, down_weight, first_moment, second_moment):
    V, DMA = pltpu.VMEM, pltpu.SemaphoreType.DMA
    pieces = (16, QUARTER)
    shapes = (
        jax.ShapeDtypeStruct((1, ROWS, D), BF16),
        jax.ShapeDtypeStruct((1, 512, UNITS), BF16),
        jax.ShapeDtypeStruct((1, 512, UNITS), BF16),
        jax.ShapeDtypeStruct((1, 512, UNITS), F32),
    )
    norm_gain = pltpu.with_memory_space_constraint(norm_gain, pltpu.HBM)
    results = pl.pallas_call(
        kernel,
        out_shape=shapes,
        in_specs=[pl.BlockSpec(memory_space=pltpu.HBM)] * 8,
        out_specs=[pl.BlockSpec(memory_space=pltpu.VMEM)] * 4,
        scratch_shapes=[
            V((ROWS, D), BF16),
            V((D, 2 * UNITS), BF16),
            V((UNITS, D), BF16),
            V((2 * UNITS, D), BF16),
            V((D, UNITS), BF16),
            V((ROWS, D), BF16),
            V((1, D), F32),
            V((512, UNITS), F32),
            V((512, UNITS), F32),
            V((ROWS, D), BF16),
            V((ROWS, UNITS), F32),
            V((ROWS, UNITS), F32),
            V((ROWS, UNITS), F32),
            V((4, ROWS, 2 * UNITS), BF16),
            V((4, ROWS, UNITS), BF16),
            V((4, ROWS, 512), BF16),
            V((4, ROWS, 512), BF16),
            V((2, 512, 2 * ROWS), BF16),
            V((2, 512, 2 * ROWS), BF16),
            V((3, 512, UNITS), F32),
            V((CHUNKS, BLOCKS) + pieces, BF16),
            V((2, TURNS, 16) + pieces, BF16),
            V((2, 16) + pieces, BF16),
            V((2, TURNS) + pieces, BF16),
            V((2,) + pieces, BF16),
            V((CHUNKS, BLOCKS) + pieces, BF16),
            V((CHUNKS, BLOCKS) + pieces, BF16),
            V((TURNS,) + pieces, BF16),
            V((2, TURNS) + pieces, BF16),
            V((2,) + pieces, BF16),
            V((2, 1, D), F32),
            V((1, D), F32),
            V((2,) + pieces, BF16),
            V((2,) + pieces, BF16),
            V((TURNS, 16, D), BF16),
            DMA((8 + TURNS,)),
            DMA((2, TURNS)),
            DMA((2,)),
            DMA((CHUNKS,)),
            DMA((CHUNKS,)),
            DMA((3,)),
            DMA((3,)),
            DMA((2,)),
            DMA((2,)),
            DMA((6,)),
            DMA((1,)),
            DMA((3,)),
            DMA((2,)),
            DMA((2,)),
            DMA((2,)),
            DMA((1,)),
            DMA((4,)),
            DMA((3,)),
        ],
        compiler_params=pltpu.CompilerParams(
            has_side_effects=True, collective_id=0, vmem_limit_bytes=50 * 1024 * 1024
        ),
        name="relay",
    )(layer_input, top_grad, norm_gain, gate_weight, up_weight, down_weight, first_moment, second_moment)
    return pl.pallas_call(
        hand_on,
        out_shape=shapes,
        in_specs=[pl.BlockSpec(memory_space=pltpu.VMEM)] * 4,
        out_specs=[pl.BlockSpec(memory_space=pltpu.HBM)] * 4,
        scratch_shapes=[DMA((4,))],
        compiler_params=pltpu.CompilerParams(vmem_limit_bytes=8 * 1024 * 1024),
        name="hand_on",
    )(*results)


def solution(mesh):
    return jax.shard_map(
        on_device,
        mesh=mesh,
        in_specs=(
            P("section", "dp", None),
            P("dp", None),
            P("section", None),
            P("section", None, "mp"),
            P("section", None, "mp"),
            P("section", "mp", None),
            P("section", "dp", "mp"),
            P("section", "dp", "mp"),
        ),
        out_specs=(
            P("section", "dp", None),
            P("section", "dp", "mp"),
            P("section", "dp", "mp"),
            P("section", "dp", "mp"),
        ),
        check_vma=False,
    )
```

```python
import jax
import jax.numpy as jnp
from jax import lax
from jax.experimental import pallas as pl
from jax.experimental.pallas import tpu as pltpu
from jax.sharding import PartitionSpec as P

first_fix = 1.0 - 0.9**20
second_fix = 1.0 - 0.95**20

MESH = pl.DeviceIdType.MESH
F32 = jnp.float32
BF16 = jnp.bfloat16

ROWS = 256
D = 2048
UNITS = 512
QUARTER = D // 4
CHUNKS = 8
CH = ROWS // CHUNKS
BLOCKS = CH // 4
TURNS = CHUNKS // 2
EARLY = 4
FAR_FIRST = (4, 3, 5, 2, 6, 1, 7, 0)
OUTER_LAST = (0, 1, 2, 7, 3, 6, 5, 4)


def dot_nn(left, right):
    return lax.dot_general(left, right, (((1,), (0,)), ((), ())), preferred_element_type=F32)


def dot_nt(left, right):
    return lax.dot_general(left, right, (((1,), (1,)), ((), ())), preferred_element_type=F32)


def swap(a, b):
    low = lax.broadcasted_iota(jnp.int32, a.shape, 0) < 4
    first = jnp.where(low, a, pltpu.roll(b, 4, 0))
    second = jnp.where(low, pltpu.roll(a, 4, 0), b)
    return first, second


def pack(quarters):
    a_top, b_top = swap(quarters[0], quarters[1])
    a_low, b_low = swap(quarters[2], quarters[3])
    return jnp.concatenate([a_top, a_low], axis=0), jnp.concatenate([b_top, b_low], axis=0)


def unpack_pair(a, b):
    first = swap(a[:8], b[:8])
    second = swap(a[8:], b[8:])
    return first + second


def row_sums(packed):
    folded = packed[:8] + packed[8:]
    folded = folded + pltpu.roll(folded, 4, 0)
    sums = jnp.sum(folded, axis=-1, keepdims=True)
    return jnp.concatenate([sums, sums], axis=0)


def quarters_of(rows):
    return [rows[:, QUARTER * q : QUARTER * (q + 1)] for q in range(4)]


def kernel(
    li_h, tg_h, gain_h, gw_h, uw_h, dw_h, fm_h, sm_h,
    ig, gg, ug, ad,
    li, w, dw, wt, dwt, up, gain, fm, sm,
    ng, gated, slope, gh, gx, hx, ngx, ux, ngt, uxt, acc,
    snd, rsbuf, rs2, rout, rout2, agbuf, igbuf,
    lisend, liown, liown2, gnown, gnown2, incb, inc2, tgown,
    ld, rs_r, rs2_r, ag_r, ig_r, li_r, gn_r, inc_r, inc2_r, dp_r,
    rs_s, ag_s, inc_s, li_s, gn_s, fw_s, dp_s, own_s,
):
    d = lax.axis_index("dp")
    s = lax.axis_index("section")
    m = lax.axis_index("mp")
    yh, z = m // 8, m % 8
    owner = jnp.where(s >= 2, 0, 3)
    turn = 1 - s % 2

    def local(src, dst, sem):
        return pltpu.make_async_copy(src, dst, sem)

    def remote(src, dst, ssem, rsem, **to):
        return pltpu.make_async_remote_copy(src, dst, ssem, rsem, device_id=to, device_id_type=MESH)

    li_load = local(li_h.at[0], li, ld.at[0])
    gain_load = local(gain_h, gain, ld.at[1])
    w_loads = []
    for j in range(2):
        cols, cols_up = pl.ds(256 * j, 256), pl.ds(UNITS + 256 * j, 256)
        gw_load = local(gw_h.at[0, :, cols], w.at[:, cols], ld.at[8 + TURNS + 2 * j])
        uw_load = local(uw_h.at[0, :, cols], w.at[:, cols_up], ld.at[9 + TURNS + 2 * j])
        w_loads.append((gw_load, uw_load))
    dw_load = local(dw_h.at[0], dw, ld.at[4])
    late = [local(fm_h.at[0], fm, ld.at[5]), local(sm_h.at[0], sm, ld.at[6])]
    tg_load = local(tg_h, up, ld.at[7])

    def own_tile(i):
        return pl.ds(pl.multiple_of(CH * (yh + 2 * i) + 16 * (z // 4), 16), 16)

    tg_rows = [local(tg_h.at[own_tile(i)], tgown.at[i], ld.at[8 + i]) for i in range(TURNS)]

    barrier = pltpu.get_barrier_semaphore()

    def greet(**to):
        pl.semaphore_signal(barrier, inc=1, device_id=to, device_id_type=MESH)

    def greet_all(section):
        def one(j, carry):
            greet(section=section, mp=j)
            return carry
        lax.fori_loop(0, 16, one, 0)

    @pl.when(s == 3)
    def _():
        greet_all(0)
        greet_all(1)
        greet_all(2)

    @pl.when(s == 2)
    def _():
        greet_all(0)
        greet(section=1)

    @pl.when(s == 1)
    def _():
        greet_all(0)
        greet_all(3)

    @pl.when(s == 0)
    def _():
        greet_all(3)
        greet_all(2)

    for k in (1, 2, 3):
        greet(dp=lax.rem(d + k, 4))

    li_load.start()
    gain_load.start()

    @pl.when(s == 3)
    def _():
        tg_load.start()

    dw_load.start()
    for gw_load, uw_load in w_loads:
        gw_load.start()
        uw_load.start()

    @pl.when(s == 0)
    def _():
        for cp in tg_rows:
            cp.start()

    for cp in late:
        cp.start()

    early, later = pl.ds(0, 2), pl.ds(2, 2)

    def own_piece(tile):
        tile = tile.astype(F32)
        rows = jnp.where((z // 2) % 2 == 0, tile[:8], tile[8:])
        a, b = pack(quarters_of(rows))
        return jnp.where(z % 2 == 0, a, b)

    li_load.wait()
    gain_load.wait()
    li_send = remote(lisend, liown.at[turn], li_s.at[0], li_r.at[turn], section=owner)
    gn_send = remote(gain, gnown.at[turn], gn_s.at[0], gn_r.at[turn], section=owner)

    def norm_rows(j, carry):
        rows = pl.ds(pl.multiple_of(j * 32, 32), 32)
        values = li[rows, :].astype(F32)
        scale_inv = lax.rsqrt(jnp.mean(values * values, axis=-1, keepdims=True) + 1e-05)
        ng[rows, :] = (values * scale_inv * gain[...]).astype(BF16)
        return carry

    lax.fori_loop(0, ROWS // 32, norm_rows, 0)
    dw_load.wait()

    @pl.when(s == 3)
    def _():
        tg_load.wait()

        def hidden_tile(j, carry):
            cols = pl.ds(pl.multiple_of(j * 256, 256), 256)
            gh[:, cols] = dot_nt(up[...], dw[cols, :])
            return carry

        lax.fori_loop(0, UNITS // 256, hidden_tile, 0)

    for i in range(TURNS):
        lisend[i] = own_piece(li[own_tile(i), :]).astype(BF16)

    for j, (gw_load, uw_load) in enumerate(w_loads):
        gw_load.wait()
        uw_load.wait()
        cols, cols_up = pl.ds(256 * j, 256), pl.ds(UNITS + 256 * j, 256)
        gate_pre = dot_nn(ng[...], w[:, cols])
        up_pre = dot_nn(ng[...], w[:, cols_up])
        sig = jax.nn.sigmoid(gate_pre)
        gate = gate_pre * sig
        gated[:, cols] = gate
        hx[0, :, cols] = (gate * up_pre).astype(BF16)
        slope[:, cols] = up_pre * sig * (1.0 + gate_pre * (1.0 - sig))

    @pl.when(s >= 2)
    def _():
        pl.semaphore_wait(barrier, 35)

    @pl.when(s == 1)
    def _():
        pl.semaphore_wait(barrier, 20)

    @pl.when(s == 0)
    def _():
        pl.semaphore_wait(barrier, 51)

    li_send.start()
    gn_send.start()
    li_later = remote(lisend.at[later], liown2, li_s.at[1], li_r.at[2], section=3)
    gn_later = remote(gain, gnown2, gn_s.at[1], gn_r.at[2], section=3)

    @pl.when(s == 2)
    def _():
        li_later.start()
        gn_later.start()

    def feature_cols(k):
        return pl.ds(pl.multiple_of(lax.rem(d + k, 4) * 512, 512), 512)

    own_ng = local(ng.at[:, feature_cols(0)], ngx.at[0], own_s.at[0])

    def bulk():
        own_ng.start()
        for k in (2, 1, 3):
            peer = lax.rem(d + k, 4)
            remote(ng.at[:, feature_cols(k)], ngx.at[4 - k], dp_s.at[0], dp_r.at[0], dp=peer).start()
            remote(hx.at[0], hx.at[4 - k], dp_s.at[1], dp_r.at[1], dp=peer).start()

    def reduce_layer(buf, sem, own_rows, own_gain, out, incoming, sends, first, stop):
        def chunk(i, carry):
            remote(buf.at[i], buf.at[i], rs_s.at[0], sem.at[i], mp=m).wait_recv()
            values = own_rows[i].astype(F32)
            scale_inv = lax.rsqrt(row_sums(values * values) * (1.0 / D) + 1e-05)
            normed = values * scale_inv
            total = buf[i, 0].astype(F32)
            for k in range(1, 16):
                total = total + buf[i, k].astype(F32)
            quarter = lax.broadcasted_iota(jnp.int32, (16, QUARTER), 0) // 4
            gain_piece = jnp.zeros((16, QUARTER), F32)
            for q in range(4):
                gain_piece = jnp.where(quarter == q, own_gain[:, pl.ds(QUARTER * q, QUARTER)], gain_piece)
            scaled = total * gain_piece
            projection = row_sums(scaled * normed) * (1.0 / D)
            out[i] = (incoming(i) + scale_inv * (scaled - normed * projection)).astype(BF16)
            sends(i)
            return carry

        lax.fori_loop(first, stop, chunk, 0)

    def reduce_turn(u, incoming, sends, first, stop):
        reduce_layer(
            rsbuf.at[u], rs_r.at[u], liown.at[u], gnown.at[u], rout.at[u], incoming, sends, first, stop
        )

    def gather_to(section, buf, sem, out, ssem, base=0, last=False):
        def sends(i):
            chunk = yh + 2 * (i + base)
            for k in FAR_FIRST:
                for h in range(2):
                    to = (OUTER_LAST[FAR_FIRST.index(k)] if last else lax.rem(z + k, 8)) + 8 * h
                    remote(out.at[i], buf.at[chunk, z], ssem, sem.at[chunk], section=section, mp=to).start()
        return sends

    def own_rows_ready(u):
        remote(liown.at[u], liown.at[u], li_s.at[0], li_r.at[u], mp=m).wait_recv()
        remote(gnown.at[u], gnown.at[u], gn_s.at[0], gn_r.at[u], mp=m).wait_recv()

    def from_rout(i):
        return rout[0, i].astype(F32)

    others = pl.ds(1, 3)

    def turn_ng():
        own_ng.wait()
        remote(ngx.at[others], ngx.at[others], dp_s.at[0], dp_r.at[0], mp=m).wait_recv()
        for h in range(2):
            for k in range(4):
                ngt[h, :, pl.ds(128 * k, 128)] = ngx[k, pl.ds(128 * h, 128), :].T

    @pl.when(s < 3)
    def _():
        bulk()

        def turn_w(j, carry):
            rows = pl.ds(pl.multiple_of(j * 256, 256), 256)
            wt[:, rows] = w[rows, :].T
            return carry

        lax.fori_loop(0, D // 256, turn_w, 0)

        def turn_dw(j, carry):
            rows = pl.ds(pl.multiple_of(j * 256, 256), 256)
            dwt[:, rows] = dw[rows, :].T
            return carry

        lax.fori_loop(0, UNITS // 256, turn_dw, 0)

    @pl.when(s == 0)
    def _():
        for cp in tg_rows:
            cp.wait()
        own_rows_ready(0)
        own_rows_ready(1)

        def from_top(i):
            return own_piece(tgown[i])

        to_two = gather_to(2, agbuf, ag_r, rout.at[0], ag_s.at[0])
        to_one = gather_to(1, agbuf, ag_r, rout.at[1], ag_s.at[1])

        def sends_three(i):
            to_two(i)

            @pl.when(i >= 2)
            def _():
                remote(rout.at[0, i], inc2.at[i % 2], inc_s.at[1], inc2_r.at[i % 2], section=3).start()

        def sends_two(i):
            to_one(i)
            remote(rout.at[1, i], incb.at[i], inc_s.at[0], inc_r.at[i], section=3).start()

        reduce_turn(0, from_top, sends_three, 0, TURNS)
        reduce_turn(1, from_rout, sends_two, 0, 2)
        turn_ng()

    below = jnp.where(s == 3, 0, s + 1)

    def unpack(src, c, dst):
        for p in range(2):
            rows = pl.ds(pl.multiple_of(CH * c + 16 * p, 16), 16)
            top = unpack_pair(src[c, 4 * p].astype(F32), src[c, 4 * p + 1].astype(F32))
            low = unpack_pair(src[c, 4 * p + 2].astype(F32), src[c, 4 * p + 3].astype(F32))
            for q in range(4):
                both = jnp.concatenate([top[q], low[q]], axis=0)
                dst[rows, pl.ds(QUARTER * q, QUARTER)] = both.astype(BF16)

    def send_partials(c, product):
        for t in range(2):
            quarters = [product(QUARTER * q + 256 * t) for q in range(4)]
            cols = pl.ds(256 * t, 256)
            for b in range(BLOCKS // 2):
                first, second = pack([x[8 * b : 8 * b + 8] for x in quarters])
                snd[c, 2 * b, :, cols] = first.astype(BF16)
                snd[c, 2 * b + 1, :, cols] = second.astype(BF16)

        moved = (s == 2) & (c >= 4)

        @pl.when(moved)
        def _():
            for k in FAR_FIRST:
                to = lax.rem(z + k, 8)
                remote(
                    snd.at[c, to], rs2.at[(c // 2) % 2, m], rs_s.at[0], rs2_r.at[(c // 2) % 2],
                    section=3, mp=to + 8 * (c % 2),
                ).start()

        @pl.when(jnp.logical_not(moved))
        def _():
            for k in FAR_FIRST:
                to = lax.rem(z + k, 8)
                remote(
                    snd.at[c, to], rsbuf.at[turn, c // 2, m], rs_s.at[0], rs_r.at[turn, c // 2],
                    section=owner, mp=to + 8 * (c % 2),
                ).start()

    def share(start, size):
        rows = pl.ds(pl.multiple_of(start, CH), size)
        half = start // 128
        local(up.at[rows, feature_cols(0)], ux.at[0, rows], own_s.at[1 + half]).start()
        for k in (2, 1, 3):
            peer = lax.rem(d + k, 4)
            remote(gx.at[0, rows], gx.at[4 - k, rows], dp_s.at[2], dp_r.at[2 + half], dp=peer).start()
            remote(up.at[rows, feature_cols(k)], ux.at[4 - k, rows], dp_s.at[3], dp_r.at[4 + half], dp=peer).start()

    @pl.when(s == 3)
    def _():
        gx[0, :, pl.ds(0, UNITS)] = (gh[...] * slope[...]).astype(BF16)
        gx[0, :, pl.ds(UNITS, UNITS)] = (gh[...] * gated[...]).astype(BF16)

        def chunk_step(c, carry):
            rows = pl.ds(pl.multiple_of(CH * c, CH), CH)
            send_partials(c, lambda at: dot_nt(gx[0, rows, :], w[pl.ds(at, 256), :]))
            return carry

        lax.fori_loop(0, CHUNKS, chunk_step, 0)
        bulk()
        share(0, 128)
        share(128, 128)

    @pl.when(s < 3)
    def _():
        def chunk_step(c, carry):
            rows = pl.ds(pl.multiple_of(CH * c, CH), CH)
            remote(agbuf.at[c], agbuf.at[c], rs_s.at[0], ag_r.at[c], mp=m).wait_recv()
            unpack(agbuf, c, up)
            grad_hidden = dot_nn(up[rows, :], dwt[...])
            gx[0, rows, pl.ds(0, UNITS)] = (grad_hidden * slope[rows, :]).astype(BF16)
            gx[0, rows, pl.ds(UNITS, UNITS)] = (grad_hidden * gated[rows, :]).astype(BF16)
            send_partials(c, lambda at: dot_nn(gx[0, rows, :], wt[:, pl.ds(at, 256)]))

            @pl.when(s == 0)
            def _():
                share(CH * c, CH)

            @pl.when((s > 0) & (c % 4 == 3))
            def _():
                share((c // 4) * 128, 128)

            @pl.when(c % 4 == 3)
            def _():
                half = pl.ds(pl.multiple_of((c // 4) * 4, 4), 4)
                remote(agbuf.at[half], igbuf.at[half], fw_s.at[0], ig_r.at[c // 4], section=below).start()

            return carry

        lax.fori_loop(0, CHUNKS, chunk_step, 0)

    @pl.when(s == 3)
    def _():
        own_rows_ready(0)
        own_rows_ready(1)
        remote(liown2, liown2, li_s.at[0], li_r.at[2], mp=m).wait_recv()
        remote(gnown2, gnown2, gn_s.at[0], gn_r.at[2], mp=m).wait_recv()

        def from_above(i):
            remote(inc2.at[i], inc2.at[i], inc_s.at[0], inc2_r.at[i], mp=m).wait_recv()
            return inc2[i].astype(F32)

        def from_inc(i):
            remote(incb.at[i], incb.at[i], inc_s.at[0], inc_r.at[i], mp=m).wait_recv()
            return incb[i].astype(F32)

        def from_later(i):
            return rout2[i % 2].astype(F32)

        to_one = gather_to(1, agbuf, ag_r, rout2, ag_s.at[2], 2)
        reduce_layer(rs2, rs2_r, liown2, gnown2, rout2, from_above, to_one, 0, 2)
        to_zero = gather_to(0, agbuf, ag_r, rout.at[0], ag_s.at[0])
        reduce_turn(0, from_inc, to_zero, 0, 2)
        reduce_turn(0, from_later, to_zero, 2, TURNS)
        reduce_turn(1, from_rout, gather_to(0, igbuf, ig_r, rout.at[1], ag_s.at[1], last=True), 0, TURNS)

    for cp in late:
        cp.wait()

    @pl.when(s > 0)
    def _():
        turn_ng()

    remote(hx.at[others], hx.at[others], dp_s.at[1], dp_r.at[1], mp=m).wait_recv()

    def last_chunk(c, carry):
        @pl.when(s == 0)
        def _():
            remote(igbuf.at[c], igbuf.at[c], rs_s.at[0], ig_r.at[c], mp=m).wait_recv()

        unpack(igbuf, c, ig.at[0])
        return carry

    for h in range(2):
        rows = pl.ds(128 * h, 128)
        local(ux.at[0, rows], ux.at[0, rows], own_s.at[1 + h]).wait()
        remote(ux.at[others, rows], ux.at[others, rows], dp_s.at[3], dp_r.at[4 + h], mp=m).wait_recv()
        for k in range(4):
            uxt[h, :, pl.ds(128 * k, 128)] = ux[k, rows, :].T
        remote(gx.at[others, rows], gx.at[others, rows], dp_s.at[2], dp_r.at[2 + h], mp=m).wait_recv()

        def grad_tile(j, carry):
            cols = pl.ds(pl.multiple_of(j * 256, 256), 256)
            cols_up = pl.ds(pl.multiple_of(UNITS + j * 256, 256), 256)
            down_sum = dot_nn(uxt[h], hx[:, rows, cols].reshape(2 * ROWS, 256))
            gate_sum = dot_nn(ngt[h], gx[:, rows, cols].reshape(2 * ROWS, 256))
            up_sum = dot_nn(ngt[h], gx[:, rows, cols_up].reshape(2 * ROWS, 256))
            if h == 0:
                acc[0, :, cols] = down_sum
                acc[1, :, cols] = gate_sum
                acc[2, :, cols] = up_sum
            else:
                down_sum = down_sum + acc[0, :, cols]
                gg[0, :, cols] = (gate_sum + acc[1, :, cols]).astype(BF16)
                ug[0, :, cols] = (up_sum + acc[2, :, cols]).astype(BF16)
                new_first = 0.9 * fm[:, cols] + 0.1 * down_sum
                new_second = 0.95 * sm[:, cols] + 0.05 * down_sum * down_sum
                ad[0, :, cols] = new_first / first_fix / (jnp.sqrt(new_second / second_fix) + 1e-08)
            return carry

        lax.fori_loop(0, UNITS // 256, grad_tile, 0)

        if h == 0:
            @pl.when(s == 0)
            def _():
                lax.fori_loop(0, EARLY, last_chunk, 0)

    @pl.when(s > 0)
    def _():
        for h in range(2):
            half = pl.ds(4 * h, 4)
            remote(igbuf.at[half], igbuf.at[half], rs_s.at[0], ig_r.at[h], mp=m).wait_recv()

    @pl.when(s > 0)
    def _():
        lax.fori_loop(0, EARLY, last_chunk, 0)

    lax.fori_loop(EARLY, CHUNKS, last_chunk, 0)

    li_send.wait_send()
    gn_send.wait_send()
    remote(snd, snd, rs_s.at[0], rs_r.at[0, 0], mp=m).wait_send()
    remote(ngx.at[others], ngx.at[others], dp_s.at[0], dp_r.at[0], mp=m).wait_send()
    remote(hx.at[others], hx.at[others], dp_s.at[1], dp_r.at[1], mp=m).wait_send()
    remote(gx.at[others], gx.at[others], dp_s.at[2], dp_r.at[2], mp=m).wait_send()
    remote(ux.at[others], ux.at[others], dp_s.at[3], dp_r.at[3], mp=m).wait_send()

    @pl.when(s < 3)
    def _():
        remote(agbuf, agbuf, fw_s.at[0], ag_r.at[0], mp=m).wait_send()

    @pl.when(s == 2)
    def _():
        li_later.wait_send()
        gn_later.wait_send()

    @pl.when(s == 0)
    def _():
        remote(rsbuf.at[0], rsbuf.at[0], ag_s.at[0], rs_r.at[0, 0], mp=m).wait_send()
        remote(rsbuf.at[1, early], rsbuf.at[1, early], ag_s.at[1], rs_r.at[0, 0], mp=m).wait_send()
        remote(rout.at[1, early], incb, inc_s.at[0], inc_r.at[0], mp=m).wait_send()
        remote(rout.at[0, later], inc2, inc_s.at[1], inc_r.at[0], mp=m).wait_send()

    @pl.when(s == 3)
    def _():
        for u in range(2):
            remote(rsbuf.at[u], rsbuf.at[u], ag_s.at[u], rs_r.at[0, 0], mp=m).wait_send()
        remote(rs2, rs2, ag_s.at[2], rs_r.at[0, 0], mp=m).wait_send()


def hand_on(*refs):
    sources, targets, sems = refs[:4], refs[4:8], refs[8]
    copies = [pltpu.make_async_copy(a, b, sems.at[i]) for i, (a, b) in enumerate(zip(sources, targets))]
    for cp in copies:
        cp.start()
    for cp in copies:
        cp.wait()


def on_device(layer_input, top_grad, norm_gain, gate_weight, up_weight, down_weight, first_moment, second_moment):
    V, DMA = pltpu.VMEM, pltpu.SemaphoreType.DMA
    pieces = (16, QUARTER)
    shapes = (
        jax.ShapeDtypeStruct((1, ROWS, D), BF16),
        jax.ShapeDtypeStruct((1, 512, UNITS), BF16),
        jax.ShapeDtypeStruct((1, 512, UNITS), BF16),
        jax.ShapeDtypeStruct((1, 512, UNITS), F32),
    )
    norm_gain = pltpu.with_memory_space_constraint(norm_gain, pltpu.HBM)
    results = pl.pallas_call(
        kernel,
        out_shape=shapes,
        in_specs=[pl.BlockSpec(memory_space=pltpu.HBM)] * 8,
        out_specs=[pl.BlockSpec(memory_space=pltpu.VMEM)] * 4,
        scratch_shapes=[
            V((ROWS, D), BF16),
            V((D, 2 * UNITS), BF16),
            V((UNITS, D), BF16),
            V((2 * UNITS, D), BF16),
            V((D, UNITS), BF16),
            V((ROWS, D), BF16),
            V((1, D), F32),
            V((512, UNITS), F32),
            V((512, UNITS), F32),
            V((ROWS, D), BF16),
            V((ROWS, UNITS), F32),
            V((ROWS, UNITS), F32),
            V((ROWS, UNITS), F32),
            V((4, ROWS, 2 * UNITS), BF16),
            V((4, ROWS, UNITS), BF16),
            V((4, ROWS, 512), BF16),
            V((4, ROWS, 512), BF16),
            V((2, 512, 2 * ROWS), BF16),
            V((2, 512, 2 * ROWS), BF16),
            V((3, 512, UNITS), F32),
            V((CHUNKS, BLOCKS) + pieces, BF16),
            V((2, TURNS, 16) + pieces, BF16),
            V((2, 16) + pieces, BF16),
            V((2, TURNS) + pieces, BF16),
            V((2,) + pieces, BF16),
            V((CHUNKS, BLOCKS) + pieces, BF16),
            V((CHUNKS, BLOCKS) + pieces, BF16),
            V((TURNS,) + pieces, BF16),
            V((2, TURNS) + pieces, BF16),
            V((2,) + pieces, BF16),
            V((2, 1, D), F32),
            V((1, D), F32),
            V((2,) + pieces, BF16),
            V((2,) + pieces, BF16),
            V((TURNS, 16, D), BF16),
            DMA((12 + TURNS,)),
            DMA((2, TURNS)),
            DMA((2,)),
            DMA((CHUNKS,)),
            DMA((CHUNKS,)),
            DMA((3,)),
            DMA((3,)),
            DMA((2,)),
            DMA((2,)),
            DMA((6,)),
            DMA((1,)),
            DMA((3,)),
            DMA((2,)),
            DMA((2,)),
            DMA((2,)),
            DMA((1,)),
            DMA((4,)),
            DMA((3,)),
        ],
        compiler_params=pltpu.CompilerParams(
            has_side_effects=True, collective_id=0, vmem_limit_bytes=50 * 1024 * 1024
        ),
        name="relay",
    )(layer_input, top_grad, norm_gain, gate_weight, up_weight, down_weight, first_moment, second_moment)
    return pl.pallas_call(
        hand_on,
        out_shape=shapes,
        in_specs=[pl.BlockSpec(memory_space=pltpu.VMEM)] * 4,
        out_specs=[pl.BlockSpec(memory_space=pltpu.HBM)] * 4,
        scratch_shapes=[DMA((4,))],
        compiler_params=pltpu.CompilerParams(vmem_limit_bytes=8 * 1024 * 1024),
        name="hand_on",
    )(*results)


def solution(mesh):
    return jax.shard_map(
        on_device,
        mesh=mesh,
        in_specs=(
            P("section", "dp", None),
            P("dp", None),
            P("section", None),
            P("section", None, "mp"),
            P("section", None, "mp"),
            P("section", "mp", None),
            P("section", "dp", "mp"),
            P("section", "dp", "mp"),
        ),
        out_specs=(
            P("section", "dp", None),
            P("section", "dp", "mp"),
            P("section", "dp", "mp"),
            P("section", "dp", "mp"),
        ),
        check_vma=False,
    )
```

```python
import jax
import jax.numpy as jnp
from jax import lax
from jax.experimental import pallas as pl
from jax.experimental.pallas import tpu as pltpu
from jax.sharding import PartitionSpec as P

first_fix = 1.0 - 0.9**20
second_fix = 1.0 - 0.95**20

MESH = pl.DeviceIdType.MESH
F32 = jnp.float32
BF16 = jnp.bfloat16

ROWS = 256
D = 2048
UNITS = 512
QUARTER = D // 4
CHUNKS = 8
CH = ROWS // CHUNKS
BLOCKS = CH // 4
TURNS = CHUNKS // 2
EARLY = 4
FAR_FIRST = (4, 3, 5, 2, 6, 1, 7, 0)
OUTER_LAST = (0, 1, 2, 7, 3, 6, 5, 4)


def dot_nn(left, right):
    return lax.dot_general(left, right, (((1,), (0,)), ((), ())), preferred_element_type=F32)


def dot_nt(left, right):
    return lax.dot_general(left, right, (((1,), (1,)), ((), ())), preferred_element_type=F32)


def swap(a, b):
    low = lax.broadcasted_iota(jnp.int32, a.shape, 0) < 4
    first = jnp.where(low, a, pltpu.roll(b, 4, 0))
    second = jnp.where(low, pltpu.roll(a, 4, 0), b)
    return first, second


def pack(quarters):
    a_top, b_top = swap(quarters[0], quarters[1])
    a_low, b_low = swap(quarters[2], quarters[3])
    return jnp.concatenate([a_top, a_low], axis=0), jnp.concatenate([b_top, b_low], axis=0)


def unpack_pair(a, b):
    first = swap(a[:8], b[:8])
    second = swap(a[8:], b[8:])
    return first + second


def row_sums(packed):
    folded = packed[:8] + packed[8:]
    folded = folded + pltpu.roll(folded, 4, 0)
    sums = jnp.sum(folded, axis=-1, keepdims=True)
    return jnp.concatenate([sums, sums], axis=0)


def quarters_of(rows):
    return [rows[:, QUARTER * q : QUARTER * (q + 1)] for q in range(4)]


def kernel(
    li_h, tg_h, gain_h, gw_h, uw_h, dw_h, fm_h, sm_h,
    ig, gg, ug, ad,
    li, w, dw, wt, dwt, up, gain, fm, sm,
    ng, gated, slope, gh, gx, hx, ngx, ux, ngt, uxt, acc,
    snd, rsbuf, rs2, rout, rout2, agbuf, igbuf,
    lisend, liown, liown2, gnown, gnown2, incb, inc2, tgown,
    ld, rs_r, rs2_r, ag_r, ig_r, li_r, gn_r, inc_r, inc2_r, dp_r,
    rs_s, ag_s, inc_s, li_s, gn_s, fw_s, dp_s, own_s,
):
    d = lax.axis_index("dp")
    s = lax.axis_index("section")
    m = lax.axis_index("mp")
    yh, z = m // 8, m % 8
    owner = jnp.where(s >= 2, 0, 3)
    turn = 1 - s % 2

    def local(src, dst, sem):
        return pltpu.make_async_copy(src, dst, sem)

    def remote(src, dst, ssem, rsem, **to):
        return pltpu.make_async_remote_copy(src, dst, ssem, rsem, device_id=to, device_id_type=MESH)

    li_load = local(li_h.at[0], li, ld.at[0])
    gain_load = local(gain_h, gain, ld.at[1])
    w_loads = []
    for j in range(2):
        cols, cols_up = pl.ds(256 * j, 256), pl.ds(UNITS + 256 * j, 256)
        gw_load = local(gw_h.at[0, :, cols], w.at[:, cols], ld.at[8 + TURNS + 2 * j])
        uw_load = local(uw_h.at[0, :, cols], w.at[:, cols_up], ld.at[9 + TURNS + 2 * j])
        w_loads.append((gw_load, uw_load))
    dw_load = local(dw_h.at[0], dw, ld.at[4])
    late = [local(fm_h.at[0], fm, ld.at[5]), local(sm_h.at[0], sm, ld.at[6])]
    tg_load = local(tg_h, up, ld.at[7])

    def own_tile(i):
        return pl.ds(pl.multiple_of(CH * (yh + 2 * i) + 16 * (z // 4), 16), 16)

    tg_rows = [local(tg_h.at[own_tile(i)], tgown.at[i], ld.at[8 + i]) for i in range(TURNS)]

    barrier = pltpu.get_barrier_semaphore()

    def greet(**to):
        pl.semaphore_signal(barrier, inc=1, device_id=to, device_id_type=MESH)

    def greet_all(section):
        def one(j, carry):
            greet(section=section, mp=j)
            return carry
        lax.fori_loop(0, 16, one, 0)

    @pl.when(s == 3)
    def _():
        greet_all(0)
        greet_all(1)
        greet_all(2)

    @pl.when(s == 2)
    def _():
        greet_all(0)
        greet(section=1)

    @pl.when(s == 1)
    def _():
        greet_all(0)
        greet_all(3)

    @pl.when(s == 0)
    def _():
        greet_all(3)
        greet_all(2)

    for k in (1, 2, 3):
        greet(dp=lax.rem(d + k, 4))

    li_load.start()
    gain_load.start()

    @pl.when(s == 3)
    def _():
        tg_load.start()

    dw_load.start()
    for gw_load, uw_load in w_loads:
        gw_load.start()
        uw_load.start()

    @pl.when(s == 0)
    def _():
        for cp in tg_rows:
            cp.start()

    for cp in late:
        cp.start()

    early, later = pl.ds(0, 2), pl.ds(2, 2)

    def own_piece(tile):
        tile = tile.astype(F32)
        rows = jnp.where((z // 2) % 2 == 0, tile[:8], tile[8:])
        a, b = pack(quarters_of(rows))
        return jnp.where(z % 2 == 0, a, b)

    li_load.wait()
    gain_load.wait()
    li_send = remote(lisend, liown.at[turn], li_s.at[0], li_r.at[turn], section=owner)
    gn_send = remote(gain, gnown.at[turn], gn_s.at[0], gn_r.at[turn], section=owner)

    def norm_rows(j, carry):
        rows = pl.ds(pl.multiple_of(j * 32, 32), 32)
        values = li[rows, :].astype(F32)
        scale_inv = lax.rsqrt(jnp.mean(values * values, axis=-1, keepdims=True) + 1e-05)
        ng[rows, :] = (values * scale_inv * gain[...]).astype(BF16)
        return carry

    lax.fori_loop(0, ROWS // 32, norm_rows, 0)
    dw_load.wait()

    @pl.when(s == 3)
    def _():
        tg_load.wait()

        def hidden_tile(j, carry):
            cols = pl.ds(pl.multiple_of(j * 256, 256), 256)
            gh[:, cols] = dot_nt(up[...], dw[cols, :])
            return carry

        lax.fori_loop(0, UNITS // 256, hidden_tile, 0)

    for i in range(TURNS):
        lisend[i] = own_piece(li[own_tile(i), :]).astype(BF16)

    for j, (gw_load, uw_load) in enumerate(w_loads):
        gw_load.wait()
        uw_load.wait()
        cols, cols_up = pl.ds(256 * j, 256), pl.ds(UNITS + 256 * j, 256)
        gate_pre = dot_nn(ng[...], w[:, cols])
        up_pre = dot_nn(ng[...], w[:, cols_up])
        sig = jax.nn.sigmoid(gate_pre)
        gate = gate_pre * sig
        gated[:, cols] = gate
        hx[0, :, cols] = (gate * up_pre).astype(BF16)
        slope[:, cols] = up_pre * sig * (1.0 + gate_pre * (1.0 - sig))

    @pl.when(s >= 2)
    def _():
        pl.semaphore_wait(barrier, 35)

    @pl.when(s == 1)
    def _():
        pl.semaphore_wait(barrier, 20)

    @pl.when(s == 0)
    def _():
        pl.semaphore_wait(barrier, 51)

    li_send.start()
    gn_send.start()
    li_later = remote(lisend.at[later], liown2, li_s.at[1], li_r.at[2], section=3)
    gn_later = remote(gain, gnown2, gn_s.at[1], gn_r.at[2], section=3)

    @pl.when(s == 2)
    def _():
        li_later.start()
        gn_later.start()

    def feature_cols(k):
        return pl.ds(pl.multiple_of(lax.rem(d + k, 4) * 512, 512), 512)

    own_ng = local(ng.at[:, feature_cols(0)], ngx.at[0], own_s.at[0])

    def bulk():
        own_ng.start()
        for k in (2, 1, 3):
            peer = lax.rem(d + k, 4)
            remote(ng.at[:, feature_cols(k)], ngx.at[4 - k], dp_s.at[0], dp_r.at[0], dp=peer).start()
            remote(hx.at[0], hx.at[4 - k], dp_s.at[1], dp_r.at[1], dp=peer).start()

    def reduce_layer(buf, sem, own_rows, own_gain, out, incoming, sends, first, stop):
        def chunk(i, carry):
            remote(buf.at[i], buf.at[i], rs_s.at[0], sem.at[i], mp=m).wait_recv()
            values = own_rows[i].astype(F32)
            scale_inv = lax.rsqrt(row_sums(values * values) * (1.0 / D) + 1e-05)
            normed = values * scale_inv
            total = buf[i, 0].astype(F32)
            for k in range(1, 16):
                total = total + buf[i, k].astype(F32)
            quarter = lax.broadcasted_iota(jnp.int32, (16, QUARTER), 0) // 4
            gain_piece = jnp.zeros((16, QUARTER), F32)
            for q in range(4):
                gain_piece = jnp.where(quarter == q, own_gain[:, pl.ds(QUARTER * q, QUARTER)], gain_piece)
            scaled = total * gain_piece
            projection = row_sums(scaled * normed) * (1.0 / D)
            out[i] = (incoming(i) + scale_inv * (scaled - normed * projection)).astype(BF16)
            sends(i)
            return carry

        lax.fori_loop(first, stop, chunk, 0)

    def reduce_turn(u, incoming, sends, first, stop):
        reduce_layer(
            rsbuf.at[u], rs_r.at[u], liown.at[u], gnown.at[u], rout.at[u], incoming, sends, first, stop
        )

    def gather_to(section, buf, sem, out, ssem, base=0, last=False):
        def sends(i):
            chunk = yh + 2 * (i + base)
            for k in FAR_FIRST:
                for h in range(2):
                    to = (OUTER_LAST[FAR_FIRST.index(k)] if last else lax.rem(z + k, 8)) + 8 * h
                    remote(out.at[i], buf.at[chunk, z], ssem, sem.at[chunk], section=section, mp=to).start()
        return sends

    def own_rows_ready(u):
        remote(liown.at[u], liown.at[u], li_s.at[0], li_r.at[u], mp=m).wait_recv()
        remote(gnown.at[u], gnown.at[u], gn_s.at[0], gn_r.at[u], mp=m).wait_recv()

    def from_rout(i):
        return rout[0, i].astype(F32)

    others = pl.ds(1, 3)

    def turn_ng():
        own_ng.wait()
        remote(ngx.at[others], ngx.at[others], dp_s.at[0], dp_r.at[0], mp=m).wait_recv()
        for h in range(2):
            size = (192, 64)[h]
            ngt[:, pl.ds(768 * h, 4 * size)] = ngx[:, pl.ds(192 * h, size), :].reshape(4 * size, 512).T

    @pl.when(s < 3)
    def _():
        bulk()

        def turn_w(j, carry):
            rows = pl.ds(pl.multiple_of(j * 256, 256), 256)
            wt[:, rows] = w[rows, :].T
            return carry

        lax.fori_loop(0, D // 256, turn_w, 0)

        def turn_dw(j, carry):
            rows = pl.ds(pl.multiple_of(j * 256, 256), 256)
            dwt[:, rows] = dw[rows, :].T
            return carry

        lax.fori_loop(0, UNITS // 256, turn_dw, 0)

    @pl.when(s == 0)
    def _():
        for cp in tg_rows:
            cp.wait()
        own_rows_ready(0)
        own_rows_ready(1)

        def from_top(i):
            return own_piece(tgown[i])

        to_two = gather_to(2, agbuf, ag_r, rout.at[0], ag_s.at[0])
        to_one = gather_to(1, agbuf, ag_r, rout.at[1], ag_s.at[1])

        def sends_three(i):
            to_two(i)

            @pl.when(i >= 2)
            def _():
                remote(rout.at[0, i], inc2.at[i % 2], inc_s.at[1], inc2_r.at[i % 2], section=3).start()

        def sends_two(i):
            to_one(i)
            remote(rout.at[1, i], incb.at[i], inc_s.at[0], inc_r.at[i], section=3).start()

        reduce_turn(0, from_top, sends_three, 0, TURNS)
        reduce_turn(1, from_rout, sends_two, 0, 2)
        turn_ng()

    below = jnp.where(s == 3, 0, s + 1)

    def unpack(src, c, dst):
        for p in range(2):
            rows = pl.ds(pl.multiple_of(CH * c + 16 * p, 16), 16)
            top = unpack_pair(src[c, 4 * p].astype(F32), src[c, 4 * p + 1].astype(F32))
            low = unpack_pair(src[c, 4 * p + 2].astype(F32), src[c, 4 * p + 3].astype(F32))
            for q in range(4):
                both = jnp.concatenate([top[q], low[q]], axis=0)
                dst[rows, pl.ds(QUARTER * q, QUARTER)] = both.astype(BF16)

    def send_partials(c, product):
        for t in range(2):
            quarters = [product(QUARTER * q + 256 * t) for q in range(4)]
            cols = pl.ds(256 * t, 256)
            for b in range(BLOCKS // 2):
                first, second = pack([x[8 * b : 8 * b + 8] for x in quarters])
                snd[c, 2 * b, :, cols] = first.astype(BF16)
                snd[c, 2 * b + 1, :, cols] = second.astype(BF16)

        moved = (s == 2) & (c >= 4)

        @pl.when(moved)
        def _():
            for k in FAR_FIRST:
                to = lax.rem(z + k, 8)
                remote(
                    snd.at[c, to], rs2.at[(c // 2) % 2, m], rs_s.at[0], rs2_r.at[(c // 2) % 2],
                    section=3, mp=to + 8 * (c % 2),
                ).start()

        @pl.when(jnp.logical_not(moved))
        def _():
            for k in FAR_FIRST:
                to = lax.rem(z + k, 8)
                remote(
                    snd.at[c, to], rsbuf.at[turn, c // 2, m], rs_s.at[0], rs_r.at[turn, c // 2],
                    section=owner, mp=to + 8 * (c % 2),
                ).start()

    def share(start, size):
        rows = pl.ds(pl.multiple_of(start, CH), size)
        half = start // 192
        local(up.at[rows, feature_cols(0)], ux.at[0, rows], own_s.at[1 + half]).start()
        for k in (2, 1, 3):
            peer = lax.rem(d + k, 4)
            remote(gx.at[0, rows], gx.at[4 - k, rows], dp_s.at[2], dp_r.at[2 + half], dp=peer).start()
            remote(up.at[rows, feature_cols(k)], ux.at[4 - k, rows], dp_s.at[3], dp_r.at[4 + half], dp=peer).start()

    @pl.when(s == 3)
    def _():
        gx[0, :, pl.ds(0, UNITS)] = (gh[...] * slope[...]).astype(BF16)
        gx[0, :, pl.ds(UNITS, UNITS)] = (gh[...] * gated[...]).astype(BF16)

        def chunk_step(c, carry):
            rows = pl.ds(pl.multiple_of(CH * c, CH), CH)
            send_partials(c, lambda at: dot_nt(gx[0, rows, :], w[pl.ds(at, 256), :]))
            return carry

        lax.fori_loop(0, CHUNKS, chunk_step, 0)
        bulk()
        share(0, 192)
        share(192, 64)

    @pl.when(s < 3)
    def _():
        def chunk_step(c, carry):
            rows = pl.ds(pl.multiple_of(CH * c, CH), CH)
            remote(agbuf.at[c], agbuf.at[c], rs_s.at[0], ag_r.at[c], mp=m).wait_recv()
            unpack(agbuf, c, up)
            grad_hidden = dot_nn(up[rows, :], dwt[...])
            gx[0, rows, pl.ds(0, UNITS)] = (grad_hidden * slope[rows, :]).astype(BF16)
            gx[0, rows, pl.ds(UNITS, UNITS)] = (grad_hidden * gated[rows, :]).astype(BF16)
            send_partials(c, lambda at: dot_nn(gx[0, rows, :], wt[:, pl.ds(at, 256)]))

            @pl.when(s == 0)
            def _():
                share(CH * c, CH)

            @pl.when((s > 0) & (c % 4 == 3))
            def _():
                share((c // 4) * 128, 64)
                share((c // 4) * 128 + 64, 64)

            @pl.when(c % 4 == 3)
            def _():
                half = pl.ds(pl.multiple_of((c // 4) * 4, 4), 4)
                remote(agbuf.at[half], igbuf.at[half], fw_s.at[0], ig_r.at[c // 4], section=below).start()

            return carry

        lax.fori_loop(0, CHUNKS, chunk_step, 0)

    @pl.when(s == 3)
    def _():
        own_rows_ready(0)
        own_rows_ready(1)
        remote(liown2, liown2, li_s.at[0], li_r.at[2], mp=m).wait_recv()
        remote(gnown2, gnown2, gn_s.at[0], gn_r.at[2], mp=m).wait_recv()

        def from_above(i):
            remote(inc2.at[i], inc2.at[i], inc_s.at[0], inc2_r.at[i], mp=m).wait_recv()
            return inc2[i].astype(F32)

        def from_inc(i):
            remote(incb.at[i], incb.at[i], inc_s.at[0], inc_r.at[i], mp=m).wait_recv()
            return incb[i].astype(F32)

        def from_later(i):
            return rout2[i % 2].astype(F32)

        to_one = gather_to(1, agbuf, ag_r, rout2, ag_s.at[2], 2)
        reduce_layer(rs2, rs2_r, liown2, gnown2, rout2, from_above, to_one, 0, 2)
        to_zero = gather_to(0, agbuf, ag_r, rout.at[0], ag_s.at[0])
        reduce_turn(0, from_inc, to_zero, 0, 2)
        reduce_turn(0, from_later, to_zero, 2, TURNS)
        reduce_turn(1, from_rout, gather_to(0, igbuf, ig_r, rout.at[1], ag_s.at[1], last=True), 0, TURNS)

    for cp in late:
        cp.wait()

    @pl.when(s > 0)
    def _():
        turn_ng()

    remote(hx.at[others], hx.at[others], dp_s.at[1], dp_r.at[1], mp=m).wait_recv()

    def last_chunk(c, carry):
        @pl.when(s == 0)
        def _():
            remote(igbuf.at[c], igbuf.at[c], rs_s.at[0], ig_r.at[c], mp=m).wait_recv()

        unpack(igbuf, c, ig.at[0])
        return carry

    for h in range(2):
        size = (192, 64)[h]
        rows, tokens = pl.ds(192 * h, size), pl.ds(768 * h, 4 * size)
        local(ux.at[0, rows], ux.at[0, rows], own_s.at[1 + h]).wait()
        remote(ux.at[others, rows], ux.at[others, rows], dp_s.at[3], dp_r.at[4 + h], mp=m).wait_recv()
        uxt[:, tokens] = ux[:, rows, :].reshape(4 * size, 512).T
        remote(gx.at[others, rows], gx.at[others, rows], dp_s.at[2], dp_r.at[2 + h], mp=m).wait_recv()

        def grad_tile(j, carry):
            cols = pl.ds(pl.multiple_of(j * 256, 256), 256)
            cols_up = pl.ds(pl.multiple_of(UNITS + j * 256, 256), 256)
            down_sum = dot_nn(uxt[:, tokens], hx[:, rows, cols].reshape(4 * size, 256))
            gate_sum = dot_nn(ngt[:, tokens], gx[:, rows, cols].reshape(4 * size, 256))
            up_sum = dot_nn(ngt[:, tokens], gx[:, rows, cols_up].reshape(4 * size, 256))
            if h == 0:
                acc[0, :, cols] = down_sum
                acc[1, :, cols] = gate_sum
                acc[2, :, cols] = up_sum
            else:
                down_sum = down_sum + acc[0, :, cols]
                gg[0, :, cols] = (gate_sum + acc[1, :, cols]).astype(BF16)
                ug[0, :, cols] = (up_sum + acc[2, :, cols]).astype(BF16)
                new_first = 0.9 * fm[:, cols] + 0.1 * down_sum
                new_second = 0.95 * sm[:, cols] + 0.05 * down_sum * down_sum
                ad[0, :, cols] = new_first / first_fix / (jnp.sqrt(new_second / second_fix) + 1e-08)
            return carry

        lax.fori_loop(0, UNITS // 256, grad_tile, 0)

        if h == 0:
            @pl.when(s == 0)
            def _():
                lax.fori_loop(0, EARLY, last_chunk, 0)

    @pl.when(s > 0)
    def _():
        for h in range(2):
            half = pl.ds(4 * h, 4)
            remote(igbuf.at[half], igbuf.at[half], rs_s.at[0], ig_r.at[h], mp=m).wait_recv()

    @pl.when(s > 0)
    def _():
        lax.fori_loop(0, EARLY, last_chunk, 0)

    lax.fori_loop(EARLY, CHUNKS, last_chunk, 0)

    li_send.wait_send()
    gn_send.wait_send()
    remote(snd, snd, rs_s.at[0], rs_r.at[0, 0], mp=m).wait_send()
    remote(ngx.at[others], ngx.at[others], dp_s.at[0], dp_r.at[0], mp=m).wait_send()
    remote(hx.at[others], hx.at[others], dp_s.at[1], dp_r.at[1], mp=m).wait_send()
    remote(gx.at[others], gx.at[others], dp_s.at[2], dp_r.at[2], mp=m).wait_send()
    remote(ux.at[others], ux.at[others], dp_s.at[3], dp_r.at[3], mp=m).wait_send()

    @pl.when(s < 3)
    def _():
        remote(agbuf, agbuf, fw_s.at[0], ag_r.at[0], mp=m).wait_send()

    @pl.when(s == 2)
    def _():
        li_later.wait_send()
        gn_later.wait_send()

    @pl.when(s == 0)
    def _():
        remote(rsbuf.at[0], rsbuf.at[0], ag_s.at[0], rs_r.at[0, 0], mp=m).wait_send()
        remote(rsbuf.at[1, early], rsbuf.at[1, early], ag_s.at[1], rs_r.at[0, 0], mp=m).wait_send()
        remote(rout.at[1, early], incb, inc_s.at[0], inc_r.at[0], mp=m).wait_send()
        remote(rout.at[0, later], inc2, inc_s.at[1], inc_r.at[0], mp=m).wait_send()

    @pl.when(s == 3)
    def _():
        for u in range(2):
            remote(rsbuf.at[u], rsbuf.at[u], ag_s.at[u], rs_r.at[0, 0], mp=m).wait_send()
        remote(rs2, rs2, ag_s.at[2], rs_r.at[0, 0], mp=m).wait_send()


def hand_on(*refs):
    sources, targets, sems = refs[:4], refs[4:8], refs[8]
    copies = [pltpu.make_async_copy(a, b, sems.at[i]) for i, (a, b) in enumerate(zip(sources, targets))]
    for cp in copies:
        cp.start()
    for cp in copies:
        cp.wait()


def on_device(layer_input, top_grad, norm_gain, gate_weight, up_weight, down_weight, first_moment, second_moment):
    V, DMA = pltpu.VMEM, pltpu.SemaphoreType.DMA
    pieces = (16, QUARTER)
    shapes = (
        jax.ShapeDtypeStruct((1, ROWS, D), BF16),
        jax.ShapeDtypeStruct((1, 512, UNITS), BF16),
        jax.ShapeDtypeStruct((1, 512, UNITS), BF16),
        jax.ShapeDtypeStruct((1, 512, UNITS), F32),
    )
    norm_gain = pltpu.with_memory_space_constraint(norm_gain, pltpu.HBM)
    results = pl.pallas_call(
        kernel,
        out_shape=shapes,
        in_specs=[pl.BlockSpec(memory_space=pltpu.HBM)] * 8,
        out_specs=[pl.BlockSpec(memory_space=pltpu.VMEM)] * 4,
        scratch_shapes=[
            V((ROWS, D), BF16),
            V((D, 2 * UNITS), BF16),
            V((UNITS, D), BF16),
            V((2 * UNITS, D), BF16),
            V((D, UNITS), BF16),
            V((ROWS, D), BF16),
            V((1, D), F32),
            V((512, UNITS), F32),
            V((512, UNITS), F32),
            V((ROWS, D), BF16),
            V((ROWS, UNITS), F32),
            V((ROWS, UNITS), F32),
            V((ROWS, UNITS), F32),
            V((4, ROWS, 2 * UNITS), BF16),
            V((4, ROWS, UNITS), BF16),
            V((4, ROWS, 512), BF16),
            V((4, ROWS, 512), BF16),
            V((512, 4 * ROWS), BF16),
            V((512, 4 * ROWS), BF16),
            V((3, 512, UNITS), F32),
            V((CHUNKS, BLOCKS) + pieces, BF16),
            V((2, TURNS, 16) + pieces, BF16),
            V((2, 16) + pieces, BF16),
            V((2, TURNS) + pieces, BF16),
            V((2,) + pieces, BF16),
            V((CHUNKS, BLOCKS) + pieces, BF16),
            V((CHUNKS, BLOCKS) + pieces, BF16),
            V((TURNS,) + pieces, BF16),
            V((2, TURNS) + pieces, BF16),
            V((2,) + pieces, BF16),
            V((2, 1, D), F32),
            V((1, D), F32),
            V((2,) + pieces, BF16),
            V((2,) + pieces, BF16),
            V((TURNS, 16, D), BF16),
            DMA((12 + TURNS,)),
            DMA((2, TURNS)),
            DMA((2,)),
            DMA((CHUNKS,)),
            DMA((CHUNKS,)),
            DMA((3,)),
            DMA((3,)),
            DMA((2,)),
            DMA((2,)),
            DMA((6,)),
            DMA((1,)),
            DMA((3,)),
            DMA((2,)),
            DMA((2,)),
            DMA((2,)),
            DMA((1,)),
            DMA((4,)),
            DMA((3,)),
        ],
        compiler_params=pltpu.CompilerParams(
            has_side_effects=True, collective_id=0, vmem_limit_bytes=50 * 1024 * 1024
        ),
        name="relay",
    )(layer_input, top_grad, norm_gain, gate_weight, up_weight, down_weight, first_moment, second_moment)
    return pl.pallas_call(
        hand_on,
        out_shape=shapes,
        in_specs=[pl.BlockSpec(memory_space=pltpu.VMEM)] * 4,
        out_specs=[pl.BlockSpec(memory_space=pltpu.HBM)] * 4,
        scratch_shapes=[DMA((4,))],
        compiler_params=pltpu.CompilerParams(vmem_limit_bytes=8 * 1024 * 1024),
        name="hand_on",
    )(*results)


def solution(mesh):
    return jax.shard_map(
        on_device,
        mesh=mesh,
        in_specs=(
            P("section", "dp", None),
            P("dp", None),
            P("section", None),
            P("section", None, "mp"),
            P("section", None, "mp"),
            P("section", "mp", None),
            P("section", "dp", "mp"),
            P("section", "dp", "mp"),
        ),
        out_specs=(
            P("section", "dp", None),
            P("section", "dp", "mp"),
            P("section", "dp", "mp"),
            P("section", "dp", "mp"),
        ),
        check_vma=False,
    )
```

```python
import jax
import jax.numpy as jnp
from jax import lax
from jax.experimental import pallas as pl
from jax.experimental.pallas import tpu as pltpu
from jax.sharding import PartitionSpec as P

first_fix = 1.0 - 0.9**20
second_fix = 1.0 - 0.95**20

MESH = pl.DeviceIdType.MESH
F32 = jnp.float32
BF16 = jnp.bfloat16

ROWS = 256
D = 2048
UNITS = 512
QUARTER = D // 4
CHUNKS = 8
CH = ROWS // CHUNKS
BLOCKS = CH // 4
TURNS = CHUNKS // 2
EARLY = 4
FAR_FIRST = (4, 3, 5, 2, 6, 1, 7, 0)
OUTER_LAST = (0, 1, 2, 7, 3, 6, 5, 4)


def dot_nn(left, right):
    return lax.dot_general(left, right, (((1,), (0,)), ((), ())), preferred_element_type=F32)


def dot_nt(left, right):
    return lax.dot_general(left, right, (((1,), (1,)), ((), ())), preferred_element_type=F32)


def swap(a, b):
    low = lax.broadcasted_iota(jnp.int32, a.shape, 0) < 4
    first = jnp.where(low, a, pltpu.roll(b, 4, 0))
    second = jnp.where(low, pltpu.roll(a, 4, 0), b)
    return first, second


def pack(quarters):
    a_top, b_top = swap(quarters[0], quarters[1])
    a_low, b_low = swap(quarters[2], quarters[3])
    return jnp.concatenate([a_top, a_low], axis=0), jnp.concatenate([b_top, b_low], axis=0)


def unpack_pair(a, b):
    first = swap(a[:8], b[:8])
    second = swap(a[8:], b[8:])
    return first + second


def row_sums(packed):
    folded = packed[:8] + packed[8:]
    folded = folded + pltpu.roll(folded, 4, 0)
    sums = jnp.sum(folded, axis=-1, keepdims=True)
    return jnp.concatenate([sums, sums], axis=0)


def quarters_of(rows):
    return [rows[:, QUARTER * q : QUARTER * (q + 1)] for q in range(4)]


def kernel(
    li_h, tg_h, gain_h, gw_h, uw_h, dw_h, fm_h, sm_h,
    ig, gg, ug, ad,
    li, w, dw, wt, dwt, up, gain, fm, sm,
    ng, gated, slope, gh, gx, hx, ngx, ux, ngt, uxt, acc,
    snd, rsbuf, rs2, rout, rout2, agbuf, igbuf,
    lisend, liown, liown2, gnown, gnown2, incb, inc2, tgown,
    ld, rs_r, rs2_r, ag_r, ig_r, li_r, gn_r, inc_r, inc2_r, dp_r,
    rs_s, ag_s, inc_s, li_s, gn_s, fw_s, dp_s, own_s,
):
    d = lax.axis_index("dp")
    s = lax.axis_index("section")
    m = lax.axis_index("mp")
    yh, z = m // 8, m % 8
    owner = jnp.where(s >= 2, 0, 3)
    turn = 1 - s % 2

    def local(src, dst, sem):
        return pltpu.make_async_copy(src, dst, sem)

    def remote(src, dst, ssem, rsem, **to):
        return pltpu.make_async_remote_copy(src, dst, ssem, rsem, device_id=to, device_id_type=MESH)

    li_load = local(li_h.at[0], li, ld.at[0])
    gain_load = local(gain_h, gain, ld.at[1])
    w_loads = []
    for j in range(2):
        cols, cols_up = pl.ds(256 * j, 256), pl.ds(UNITS + 256 * j, 256)
        gw_load = local(gw_h.at[0, :, cols], w.at[:, cols], ld.at[8 + TURNS + 2 * j])
        uw_load = local(uw_h.at[0, :, cols], w.at[:, cols_up], ld.at[9 + TURNS + 2 * j])
        w_loads.append((gw_load, uw_load))
    dw_load = local(dw_h.at[0], dw, ld.at[4])
    late = [local(fm_h.at[0], fm, ld.at[5]), local(sm_h.at[0], sm, ld.at[6])]
    tg_load = local(tg_h, up, ld.at[7])

    def own_tile(i):
        return pl.ds(pl.multiple_of(CH * (yh + 2 * i) + 16 * (z // 4), 16), 16)

    tg_rows = [local(tg_h.at[own_tile(i)], tgown.at[i], ld.at[8 + i]) for i in range(TURNS)]

    barrier = pltpu.get_barrier_semaphore()

    def greet(**to):
        pl.semaphore_signal(barrier, inc=1, device_id=to, device_id_type=MESH)

    def greet_all(section):
        def one(j, carry):
            greet(section=section, mp=j)
            return carry
        lax.fori_loop(0, 16, one, 0)

    @pl.when(s == 3)
    def _():
        greet_all(0)
        greet_all(1)
        greet_all(2)

    @pl.when(s == 2)
    def _():
        greet_all(0)
        greet(section=1)

    @pl.when(s == 1)
    def _():
        greet_all(0)
        greet_all(3)

    @pl.when(s == 0)
    def _():
        greet_all(3)
        greet_all(2)

    for k in (1, 2, 3):
        greet(dp=lax.rem(d + k, 4))

    li_load.start()
    gain_load.start()

    @pl.when(s == 3)
    def _():
        tg_load.start()

    dw_load.start()
    for gw_load, uw_load in w_loads:
        gw_load.start()
        uw_load.start()

    @pl.when(s == 0)
    def _():
        for cp in tg_rows:
            cp.start()

    for cp in late:
        cp.start()

    early, later = pl.ds(0, 2), pl.ds(2, 2)

    def own_piece(tile):
        tile = tile.astype(F32)
        rows = jnp.where((z // 2) % 2 == 0, tile[:8], tile[8:])
        a, b = pack(quarters_of(rows))
        return jnp.where(z % 2 == 0, a, b)

    li_load.wait()
    gain_load.wait()
    li_send = remote(lisend, liown.at[turn], li_s.at[0], li_r.at[turn], section=owner)
    gn_send = remote(gain, gnown.at[turn], gn_s.at[0], gn_r.at[turn], section=owner)

    def norm_rows(j, carry):
        rows = pl.ds(pl.multiple_of(j * 32, 32), 32)
        values = li[rows, :].astype(F32)
        scale_inv = lax.rsqrt(jnp.mean(values * values, axis=-1, keepdims=True) + 1e-05)
        ng[rows, :] = (values * scale_inv * gain[...]).astype(BF16)
        return carry

    lax.fori_loop(0, ROWS // 32, norm_rows, 0)
    dw_load.wait()

    @pl.when(s == 3)
    def _():
        tg_load.wait()

        def hidden_tile(j, carry):
            cols = pl.ds(pl.multiple_of(j * 256, 256), 256)
            gh[:, cols] = dot_nt(up[...], dw[cols, :])
            return carry

        lax.fori_loop(0, UNITS // 256, hidden_tile, 0)

    for i in range(TURNS):
        lisend[i] = own_piece(li[own_tile(i), :]).astype(BF16)

    for j, (gw_load, uw_load) in enumerate(w_loads):
        gw_load.wait()
        uw_load.wait()
        cols, cols_up = pl.ds(256 * j, 256), pl.ds(UNITS + 256 * j, 256)
        gate_pre = dot_nn(ng[...], w[:, cols])
        up_pre = dot_nn(ng[...], w[:, cols_up])
        sig = jax.nn.sigmoid(gate_pre)
        gate = gate_pre * sig
        gated[:, cols] = gate
        hx[0, :, cols] = (gate * up_pre).astype(BF16)
        slope[:, cols] = up_pre * sig * (1.0 + gate_pre * (1.0 - sig))

    @pl.when(s >= 2)
    def _():
        pl.semaphore_wait(barrier, 35)

    @pl.when(s == 1)
    def _():
        pl.semaphore_wait(barrier, 20)

    @pl.when(s == 0)
    def _():
        pl.semaphore_wait(barrier, 51)

    li_send.start()
    gn_send.start()
    li_later = remote(lisend.at[later], liown2, li_s.at[1], li_r.at[2], section=3)
    gn_later = remote(gain, gnown2, gn_s.at[1], gn_r.at[2], section=3)

    @pl.when(s == 2)
    def _():
        li_later.start()
        gn_later.start()

    def feature_cols(k):
        return pl.ds(pl.multiple_of(lax.rem(d + k, 4) * 512, 512), 512)

    own_ng = local(ng.at[:, feature_cols(0)], ngx.at[0], own_s.at[0])

    def bulk():
        own_ng.start()
        for k in (2, 1, 3):
            peer = lax.rem(d + k, 4)
            remote(ng.at[:, feature_cols(k)], ngx.at[4 - k], dp_s.at[0], dp_r.at[0], dp=peer).start()
            remote(hx.at[0], hx.at[4 - k], dp_s.at[1], dp_r.at[1], dp=peer).start()

    def reduce_layer(buf, sem, own_rows, own_gain, out, incoming, sends, first, stop):
        def chunk(i, carry):
            remote(buf.at[i], buf.at[i], rs_s.at[0], sem.at[i], mp=m).wait_recv()
            values = own_rows[i].astype(F32)
            scale_inv = lax.rsqrt(row_sums(values * values) * (1.0 / D) + 1e-05)
            normed = values * scale_inv
            total = buf[i, 0].astype(F32)
            for k in range(1, 16):
                total = total + buf[i, k].astype(F32)
            quarter = lax.broadcasted_iota(jnp.int32, (16, QUARTER), 0) // 4
            gain_piece = jnp.zeros((16, QUARTER), F32)
            for q in range(4):
                gain_piece = jnp.where(quarter == q, own_gain[:, pl.ds(QUARTER * q, QUARTER)], gain_piece)
            scaled = total * gain_piece
            projection = row_sums(scaled * normed) * (1.0 / D)
            out[i] = (incoming(i) + scale_inv * (scaled - normed * projection)).astype(BF16)
            sends(i)
            return carry

        lax.fori_loop(first, stop, chunk, 0)

    def reduce_turn(u, incoming, sends, first, stop):
        reduce_layer(
            rsbuf.at[u], rs_r.at[u], liown.at[u], gnown.at[u], rout.at[u], incoming, sends, first, stop
        )

    def gather_to(section, buf, sem, out, ssem, base=0, last=False):
        def sends(i):
            chunk = yh + 2 * (i + base)
            for k in FAR_FIRST:
                for h in range(2):
                    to = (OUTER_LAST[FAR_FIRST.index(k)] if last else lax.rem(z + k, 8)) + 8 * h
                    remote(out.at[i], buf.at[chunk, z], ssem, sem.at[chunk], section=section, mp=to).start()
        return sends

    def own_rows_ready(u):
        remote(liown.at[u], liown.at[u], li_s.at[0], li_r.at[u], mp=m).wait_recv()
        remote(gnown.at[u], gnown.at[u], gn_s.at[0], gn_r.at[u], mp=m).wait_recv()

    def from_rout(i):
        return rout[0, i].astype(F32)

    others = pl.ds(1, 3)

    def turn_ng():
        own_ng.wait()
        remote(ngx.at[others], ngx.at[others], dp_s.at[0], dp_r.at[0], mp=m).wait_recv()
        for h in range(2):
            size = (224, 32)[h]
            ngt[:, pl.ds(896 * h, 4 * size)] = ngx[:, pl.ds(224 * h, size), :].reshape(4 * size, 512).T

    @pl.when(s < 3)
    def _():
        bulk()

        def turn_w(j, carry):
            rows = pl.ds(pl.multiple_of(j * 256, 256), 256)
            wt[:, rows] = w[rows, :].T
            return carry

        lax.fori_loop(0, D // 256, turn_w, 0)

        def turn_dw(j, carry):
            rows = pl.ds(pl.multiple_of(j * 256, 256), 256)
            dwt[:, rows] = dw[rows, :].T
            return carry

        lax.fori_loop(0, UNITS // 256, turn_dw, 0)

    @pl.when(s == 0)
    def _():
        for cp in tg_rows:
            cp.wait()
        own_rows_ready(0)
        own_rows_ready(1)

        def from_top(i):
            return own_piece(tgown[i])

        to_two = gather_to(2, agbuf, ag_r, rout.at[0], ag_s.at[0])
        to_one = gather_to(1, agbuf, ag_r, rout.at[1], ag_s.at[1])

        def sends_three(i):
            to_two(i)

            @pl.when(i >= 2)
            def _():
                remote(rout.at[0, i], inc2.at[i % 2], inc_s.at[1], inc2_r.at[i % 2], section=3).start()

        def sends_two(i):
            to_one(i)
            remote(rout.at[1, i], incb.at[i], inc_s.at[0], inc_r.at[i], section=3).start()

        reduce_turn(0, from_top, sends_three, 0, TURNS)
        reduce_turn(1, from_rout, sends_two, 0, 2)
        turn_ng()

    below = jnp.where(s == 3, 0, s + 1)

    def unpack(src, c, dst):
        for p in range(2):
            rows = pl.ds(pl.multiple_of(CH * c + 16 * p, 16), 16)
            top = unpack_pair(src[c, 4 * p].astype(F32), src[c, 4 * p + 1].astype(F32))
            low = unpack_pair(src[c, 4 * p + 2].astype(F32), src[c, 4 * p + 3].astype(F32))
            for q in range(4):
                both = jnp.concatenate([top[q], low[q]], axis=0)
                dst[rows, pl.ds(QUARTER * q, QUARTER)] = both.astype(BF16)

    def send_partials(c, product):
        for t in range(2):
            quarters = [product(QUARTER * q + 256 * t) for q in range(4)]
            cols = pl.ds(256 * t, 256)
            for b in range(BLOCKS // 2):
                first, second = pack([x[8 * b : 8 * b + 8] for x in quarters])
                snd[c, 2 * b, :, cols] = first.astype(BF16)
                snd[c, 2 * b + 1, :, cols] = second.astype(BF16)

        moved = (s == 2) & (c >= 4)

        @pl.when(moved)
        def _():
            for k in FAR_FIRST:
                to = lax.rem(z + k, 8)
                remote(
                    snd.at[c, to], rs2.at[(c // 2) % 2, m], rs_s.at[0], rs2_r.at[(c // 2) % 2],
                    section=3, mp=to + 8 * (c % 2),
                ).start()

        @pl.when(jnp.logical_not(moved))
        def _():
            for k in FAR_FIRST:
                to = lax.rem(z + k, 8)
                remote(
                    snd.at[c, to], rsbuf.at[turn, c // 2, m], rs_s.at[0], rs_r.at[turn, c // 2],
                    section=owner, mp=to + 8 * (c % 2),
                ).start()

    def share(start, size):
        rows = pl.ds(pl.multiple_of(start, CH), size)
        half = start // 224
        local(up.at[rows, feature_cols(0)], ux.at[0, rows], own_s.at[1 + half]).start()
        for k in (2, 1, 3):
            peer = lax.rem(d + k, 4)
            remote(gx.at[0, rows], gx.at[4 - k, rows], dp_s.at[2], dp_r.at[2 + half], dp=peer).start()
            remote(up.at[rows, feature_cols(k)], ux.at[4 - k, rows], dp_s.at[3], dp_r.at[4 + half], dp=peer).start()

    @pl.when(s == 3)
    def _():
        gx[0, :, pl.ds(0, UNITS)] = (gh[...] * slope[...]).astype(BF16)
        gx[0, :, pl.ds(UNITS, UNITS)] = (gh[...] * gated[...]).astype(BF16)

        def chunk_step(c, carry):
            rows = pl.ds(pl.multiple_of(CH * c, CH), CH)
            send_partials(c, lambda at: dot_nt(gx[0, rows, :], w[pl.ds(at, 256), :]))
            return carry

        lax.fori_loop(0, CHUNKS, chunk_step, 0)
        bulk()
        share(0, 224)
        share(224, 32)

    @pl.when(s < 3)
    def _():
        def chunk_step(c, carry):
            rows = pl.ds(pl.multiple_of(CH * c, CH), CH)
            remote(agbuf.at[c], agbuf.at[c], rs_s.at[0], ag_r.at[c], mp=m).wait_recv()
            unpack(agbuf, c, up)
            grad_hidden = dot_nn(up[rows, :], dwt[...])
            gx[0, rows, pl.ds(0, UNITS)] = (grad_hidden * slope[rows, :]).astype(BF16)
            gx[0, rows, pl.ds(UNITS, UNITS)] = (grad_hidden * gated[rows, :]).astype(BF16)
            send_partials(c, lambda at: dot_nn(gx[0, rows, :], wt[:, pl.ds(at, 256)]))

            @pl.when(s == 0)
            def _():
                share(CH * c, CH)

            @pl.when((s > 0) & (c % 4 == 3))
            def _():
                share((c // 4) * 128, 64)
                share((c // 4) * 128 + 64, 32)
                share((c // 4) * 128 + 96, 32)

            @pl.when(c % 4 == 3)
            def _():
                half = pl.ds(pl.multiple_of((c // 4) * 4, 4), 4)
                remote(agbuf.at[half], igbuf.at[half], fw_s.at[0], ig_r.at[c // 4], section=below).start()

            return carry

        lax.fori_loop(0, CHUNKS, chunk_step, 0)

    @pl.when(s == 3)
    def _():
        own_rows_ready(0)
        own_rows_ready(1)
        remote(liown2, liown2, li_s.at[0], li_r.at[2], mp=m).wait_recv()
        remote(gnown2, gnown2, gn_s.at[0], gn_r.at[2], mp=m).wait_recv()

        def from_above(i):
            remote(inc2.at[i], inc2.at[i], inc_s.at[0], inc2_r.at[i], mp=m).wait_recv()
            return inc2[i].astype(F32)

        def from_inc(i):
            remote(incb.at[i], incb.at[i], inc_s.at[0], inc_r.at[i], mp=m).wait_recv()
            return incb[i].astype(F32)

        def from_later(i):
            return rout2[i % 2].astype(F32)

        to_one = gather_to(1, agbuf, ag_r, rout2, ag_s.at[2], 2)
        reduce_layer(rs2, rs2_r, liown2, gnown2, rout2, from_above, to_one, 0, 2)
        to_zero = gather_to(0, agbuf, ag_r, rout.at[0], ag_s.at[0])
        reduce_turn(0, from_inc, to_zero, 0, 2)
        reduce_turn(0, from_later, to_zero, 2, TURNS)
        reduce_turn(1, from_rout, gather_to(0, igbuf, ig_r, rout.at[1], ag_s.at[1], last=True), 0, TURNS)

    for cp in late:
        cp.wait()

    @pl.when(s > 0)
    def _():
        turn_ng()

    remote(hx.at[others], hx.at[others], dp_s.at[1], dp_r.at[1], mp=m).wait_recv()

    def last_chunk(c, carry):
        @pl.when(s == 0)
        def _():
            remote(igbuf.at[c], igbuf.at[c], rs_s.at[0], ig_r.at[c], mp=m).wait_recv()

        unpack(igbuf, c, ig.at[0])
        return carry

    for h in range(2):
        size = (224, 32)[h]
        rows, tokens = pl.ds(224 * h, size), pl.ds(896 * h, 4 * size)
        local(ux.at[0, rows], ux.at[0, rows], own_s.at[1 + h]).wait()
        remote(ux.at[others, rows], ux.at[others, rows], dp_s.at[3], dp_r.at[4 + h], mp=m).wait_recv()
        uxt[:, tokens] = ux[:, rows, :].reshape(4 * size, 512).T
        remote(gx.at[others, rows], gx.at[others, rows], dp_s.at[2], dp_r.at[2 + h], mp=m).wait_recv()

        def grad_tile(j, carry):
            cols = pl.ds(pl.multiple_of(j * 256, 256), 256)
            cols_up = pl.ds(pl.multiple_of(UNITS + j * 256, 256), 256)
            down_sum = dot_nn(uxt[:, tokens], hx[:, rows, cols].reshape(4 * size, 256))
            gate_sum = dot_nn(ngt[:, tokens], gx[:, rows, cols].reshape(4 * size, 256))
            up_sum = dot_nn(ngt[:, tokens], gx[:, rows, cols_up].reshape(4 * size, 256))
            if h == 0:
                acc[0, :, cols] = down_sum
                acc[1, :, cols] = gate_sum
                acc[2, :, cols] = up_sum
            else:
                down_sum = down_sum + acc[0, :, cols]
                gg[0, :, cols] = (gate_sum + acc[1, :, cols]).astype(BF16)
                ug[0, :, cols] = (up_sum + acc[2, :, cols]).astype(BF16)
                new_first = 0.9 * fm[:, cols] + 0.1 * down_sum
                new_second = 0.95 * sm[:, cols] + 0.05 * down_sum * down_sum
                ad[0, :, cols] = new_first / first_fix / (jnp.sqrt(new_second / second_fix) + 1e-08)
            return carry

        lax.fori_loop(0, UNITS // 256, grad_tile, 0)

        if h == 0:
            @pl.when(s == 0)
            def _():
                lax.fori_loop(0, EARLY, last_chunk, 0)

    @pl.when(s > 0)
    def _():
        for h in range(2):
            half = pl.ds(4 * h, 4)
            remote(igbuf.at[half], igbuf.at[half], rs_s.at[0], ig_r.at[h], mp=m).wait_recv()

    @pl.when(s > 0)
    def _():
        lax.fori_loop(0, EARLY, last_chunk, 0)

    lax.fori_loop(EARLY, CHUNKS, last_chunk, 0)

    li_send.wait_send()
    gn_send.wait_send()
    remote(snd, snd, rs_s.at[0], rs_r.at[0, 0], mp=m).wait_send()
    remote(ngx.at[others], ngx.at[others], dp_s.at[0], dp_r.at[0], mp=m).wait_send()
    remote(hx.at[others], hx.at[others], dp_s.at[1], dp_r.at[1], mp=m).wait_send()
    remote(gx.at[others], gx.at[others], dp_s.at[2], dp_r.at[2], mp=m).wait_send()
    remote(ux.at[others], ux.at[others], dp_s.at[3], dp_r.at[3], mp=m).wait_send()

    @pl.when(s < 3)
    def _():
        remote(agbuf, agbuf, fw_s.at[0], ag_r.at[0], mp=m).wait_send()

    @pl.when(s == 2)
    def _():
        li_later.wait_send()
        gn_later.wait_send()

    @pl.when(s == 0)
    def _():
        remote(rsbuf.at[0], rsbuf.at[0], ag_s.at[0], rs_r.at[0, 0], mp=m).wait_send()
        remote(rsbuf.at[1, early], rsbuf.at[1, early], ag_s.at[1], rs_r.at[0, 0], mp=m).wait_send()
        remote(rout.at[1, early], incb, inc_s.at[0], inc_r.at[0], mp=m).wait_send()
        remote(rout.at[0, later], inc2, inc_s.at[1], inc_r.at[0], mp=m).wait_send()

    @pl.when(s == 3)
    def _():
        for u in range(2):
            remote(rsbuf.at[u], rsbuf.at[u], ag_s.at[u], rs_r.at[0, 0], mp=m).wait_send()
        remote(rs2, rs2, ag_s.at[2], rs_r.at[0, 0], mp=m).wait_send()


def hand_on(*refs):
    sources, targets, sems = refs[:4], refs[4:8], refs[8]
    copies = [pltpu.make_async_copy(a, b, sems.at[i]) for i, (a, b) in enumerate(zip(sources, targets))]
    for cp in copies:
        cp.start()
    for cp in copies:
        cp.wait()


def on_device(layer_input, top_grad, norm_gain, gate_weight, up_weight, down_weight, first_moment, second_moment):
    V, DMA = pltpu.VMEM, pltpu.SemaphoreType.DMA
    pieces = (16, QUARTER)
    shapes = (
        jax.ShapeDtypeStruct((1, ROWS, D), BF16),
        jax.ShapeDtypeStruct((1, 512, UNITS), BF16),
        jax.ShapeDtypeStruct((1, 512, UNITS), BF16),
        jax.ShapeDtypeStruct((1, 512, UNITS), F32),
    )
    norm_gain = pltpu.with_memory_space_constraint(norm_gain, pltpu.HBM)
    results = pl.pallas_call(
        kernel,
        out_shape=shapes,
        in_specs=[pl.BlockSpec(memory_space=pltpu.HBM)] * 8,
        out_specs=[pl.BlockSpec(memory_space=pltpu.VMEM)] * 4,
        scratch_shapes=[
            V((ROWS, D), BF16),
            V((D, 2 * UNITS), BF16),
            V((UNITS, D), BF16),
            V((2 * UNITS, D), BF16),
            V((D, UNITS), BF16),
            V((ROWS, D), BF16),
            V((1, D), F32),
            V((512, UNITS), F32),
            V((512, UNITS), F32),
            V((ROWS, D), BF16),
            V((ROWS, UNITS), F32),
            V((ROWS, UNITS), F32),
            V((ROWS, UNITS), F32),
            V((4, ROWS, 2 * UNITS), BF16),
            V((4, ROWS, UNITS), BF16),
            V((4, ROWS, 512), BF16),
            V((4, ROWS, 512), BF16),
            V((512, 4 * ROWS), BF16),
            V((512, 4 * ROWS), BF16),
            V((3, 512, UNITS), F32),
            V((CHUNKS, BLOCKS) + pieces, BF16),
            V((2, TURNS, 16) + pieces, BF16),
            V((2, 16) + pieces, BF16),
            V((2, TURNS) + pieces, BF16),
            V((2,) + pieces, BF16),
            V((CHUNKS, BLOCKS) + pieces, BF16),
            V((CHUNKS, BLOCKS) + pieces, BF16),
            V((TURNS,) + pieces, BF16),
            V((2, TURNS) + pieces, BF16),
            V((2,) + pieces, BF16),
            V((2, 1, D), F32),
            V((1, D), F32),
            V((2,) + pieces, BF16),
            V((2,) + pieces, BF16),
            V((TURNS, 16, D), BF16),
            DMA((12 + TURNS,)),
            DMA((2, TURNS)),
            DMA((2,)),
            DMA((CHUNKS,)),
            DMA((CHUNKS,)),
            DMA((3,)),
            DMA((3,)),
            DMA((2,)),
            DMA((2,)),
            DMA((6,)),
            DMA((1,)),
            DMA((3,)),
            DMA((2,)),
            DMA((2,)),
            DMA((2,)),
            DMA((1,)),
            DMA((4,)),
            DMA((3,)),
        ],
        compiler_params=pltpu.CompilerParams(
            has_side_effects=True, collective_id=0, vmem_limit_bytes=50 * 1024 * 1024
        ),
        name="relay",
    )(layer_input, top_grad, norm_gain, gate_weight, up_weight, down_weight, first_moment, second_moment)
    return pl.pallas_call(
        hand_on,
        out_shape=shapes,
        in_specs=[pl.BlockSpec(memory_space=pltpu.VMEM)] * 4,
        out_specs=[pl.BlockSpec(memory_space=pltpu.HBM)] * 4,
        scratch_shapes=[DMA((4,))],
        compiler_params=pltpu.CompilerParams(vmem_limit_bytes=8 * 1024 * 1024),
        name="hand_on",
    )(*results)


def solution(mesh):
    return jax.shard_map(
        on_device,
        mesh=mesh,
        in_specs=(
            P("section", "dp", None),
            P("dp", None),
            P("section", None),
            P("section", None, "mp"),
            P("section", None, "mp"),
            P("section", "mp", None),
            P("section", "dp", "mp"),
            P("section", "dp", "mp"),
        ),
        out_specs=(
            P("section", "dp", None),
            P("section", "dp", "mp"),
            P("section", "dp", "mp"),
            P("section", "dp", "mp"),
        ),
        check_vma=False,
    )
```
